256 devices in a mesh: blk: 32 (over z, y_hi, core), head: 8 (over x, y_lo).
Axes of the slice: x: 4, y: 4 (y_hi: 2, y_lo: 2; y = y_hi * 2 + y_lo), z: 8, core: 2. Of those that a mesh axis runs over, the one named last changes fastest.
Arguments:
- query_nope: bfloat16 [2048, 16384], P('blk', 'head'), may hold values from -6 to 6
- query_rope: bfloat16 [2048, 8192], P('blk', 'head'), may hold values from -16 to 16
- key_absorb: bfloat16 [128, 128, 512], P('head'), may hold values from -0.5 to 0.5
- value_absorb: bfloat16 [128, 512, 128], P('head'), may hold values from -0.25 to 0.25
- out_weight: bfloat16 [16384, 7168], P('head', 'blk'), may hold values from -0.046875 to 0.046875
- latent_cache: bfloat16 [512, 4096], P(None, 'blk'), may hold values from -9 to 9
- rope_key: bfloat16 [64, 4096], P(None, 'blk'), may hold values from -6 to 6
Outputs:
- answers: bfloat16 [2048, 7168], P('head', 'blk')
The draws below stay inside these ranges and needn't reach their ends.
All inputs are finite; a program needn't handle non-finite values.
Results may differ from the reference program's by a relative error of at most 0.019.
Values may be sent and summed in bfloat16 or wider, within the bound.
A program may use at most 128 MiB of HBM per device.

```python
import jax
import jax.numpy as jnp
from jax import lax

H = 128
NOPE = 128
ROPE = 64
LAT = 512
VD = 128
D = 7168
QTOT = 2048
DOC = 4096


def draw_rope_key(key, part):
    key = jax.random.fold_in(key, 11)
    values = jnp.clip(jax.random.normal(key, (ROPE, DOC), jnp.float32), -6.0, 6.0)
    return values.astype(jnp.bfloat16)


def draw_query_rope(key, part):
    key = jax.random.fold_in(key, 23)
    values = jnp.clip(jax.random.normal(key, (QTOT, H * ROPE), jnp.float32), -6.0, 6.0)
    return values.astype(jnp.bfloat16)


def levels(rng, dims, split, smallest, top_value):
    def one(dim, blocks):
        draws = jax.random.uniform(jax.random.fold_in(jax.random.fold_in(rng, 6), dim), (blocks,), jnp.float32, smallest / len(split), top_value / len(split))
        return jnp.repeat(jnp.exp(draws), dims[dim] // blocks).reshape((-1,) + (1,) * (len(dims) - dim - 1))

    gain = one(*split[0])
    for cut in split[1:]:
        gain = gain * one(*cut)
    return gain


def noise(own_key, dims, spread, bound, shards=(), dtype=jnp.bfloat16):
    drawn = jax.random.normal(own_key, dims, jnp.float32) * spread
    if len(shards) > 0:
        drawn = levels(own_key, dims, shards, -0.22, 0.18) * drawn
    return jnp.clip(drawn, min=-bound, max=bound).astype(dtype)


def setup_inputs(seed: int = 0) -> dict:
    seeds = jax.random.split(jax.random.key(seed), 8)
    return {
        "query_nope": noise(seeds[0], (QTOT, H * NOPE), 1.0, 6.0, ((0, 32), (1, 8))),
        "query_rope": draw_query_rope(jax.random.fold_in(seeds[7], 71), 0),
        "key_absorb": noise(seeds[2], (H, NOPE, LAT), NOPE ** -0.5, 0.5, ((0, 8),)),
        "value_absorb": noise(seeds[3], (H, LAT, VD), LAT ** -0.5, 0.25, ((0, 8),)),
        "out_weight": noise(seeds[4], (H * VD, D), (H * VD) ** -0.5, 0.046875, ((0, 8), (1, 32))),
        "latent_cache": noise(seeds[5], (LAT, DOC), 1.5, 9.0, ((1, 32),)),
        "rope_key": draw_rope_key(jax.random.fold_in(seeds[7], 71), 0),
    }


def head_output(inputs, latent_cache, rope_key):
    nope_part, rope_part, key_part, value_part = inputs
    absorbed = jnp.dot(nope_part, key_part, preferred_element_type=jnp.float32).astype(jnp.bfloat16)
    score_scale = (NOPE + ROPE) ** -0.5
    scores = (jnp.dot(absorbed, latent_cache, preferred_element_type=jnp.float32)
              + jnp.dot(rope_part, rope_key, preferred_element_type=jnp.float32)) * score_scale
    row_max = jnp.max(scores, axis=1, keepdims=True)
    weights = jnp.exp(scores - row_max)
    row_sum = jnp.sum(weights, axis=1, keepdims=True)
    mixture = lax.dot_general(weights.astype(jnp.bfloat16), latent_cache, (((1,), (1,)), ((), ())),
                              preferred_element_type=jnp.float32) / row_sum
    mixture = mixture.astype(jnp.bfloat16)
    return jnp.dot(mixture, value_part, preferred_element_type=jnp.float32).astype(jnp.bfloat16)


def reference(query_nope, query_rope, key_absorb, value_absorb, out_weight, latent_cache, rope_key):
    nope_heads = query_nope.reshape(QTOT, H, NOPE).transpose(1, 0, 2)
    rope_heads = query_rope.reshape(QTOT, H, ROPE).transpose(1, 0, 2)

    def per_head(inputs):
        return head_output(inputs, latent_cache, rope_key)

    outputs = lax.map(per_head, (nope_heads, rope_heads, key_absorb, value_absorb))
    attended = outputs.transpose(1, 0, 2).reshape(QTOT, H * VD)
    return jnp.dot(attended, out_weight, preferred_element_type=jnp.float32).astype(jnp.bfloat16)
```

```python
import functools
import math

import jax
import jax.numpy as jnp
from jax import lax
from jax.experimental import pallas as pl
from jax.experimental.pallas import tpu as pltpu
from jax.sharding import PartitionSpec as P

MESH = pl.DeviceIdType.MESH
F32 = jnp.float32
BF16 = jnp.bfloat16

Z = 8
X = 4
GROUPS = 4


def flip(value, bit):
    return value + bit - 2 * bit * (value // bit % 2)


def kernel(
    qn_hbm, qr_hbm, ka_hbm, va_hbm, w_hbm, lat_hbm, rk_hbm, out_ref,
    keys, queries, qn, qr, ka, va, weight, relay, scores, lane_max, lane_sum, acc,
    att, part, summed,
    local_sem, key_send, key_recv, w_send, w_recv, att_send, att_recv, out_send, out_recv,
):
    blk = lax.axis_index("blk")
    head = lax.axis_index("head")
    z = blk // 4
    mine = blk % 4
    yhi = mine // 2
    core = blk % 2
    x = head // 2
    sibling = flip(blk, 1)
    other_y = flip(blk, 2)
    head_y = flip(head, 1)
    side = 1 - 2 * core

    lat = lat_hbm.shape[0]
    rope = rk_hbm.shape[0]
    heads, nope = ka_hbm.shape[0], ka_hbm.shape[1]
    vd = va_hbm.shape[2]
    rows = qn_hbm.shape[0]
    pairs = heads * rows
    group_heads = heads // GROUPS
    group_rows = group_heads * rows
    factor = (nope + rope) ** (-0.5) * math.log2(math.e)

    def wrap_z(value):
        return (value + 2 * Z) % Z

    def at_z(step):
        return wrap_z(z + step) * 4 + mine

    def at_x(step):
        return (x + step + X) % X * 2 + head % 2

    loads = [
        pltpu.make_async_copy(lat_hbm, keys.at[blk, pl.ds(0, lat)], local_sem.at[0]),
        pltpu.make_async_copy(rk_hbm, keys.at[blk, pl.ds(lat, rope)], local_sem.at[1]),
        pltpu.make_async_copy(qn_hbm, qn, local_sem.at[2]),
        pltpu.make_async_copy(qr_hbm, qr, local_sem.at[3]),
        pltpu.make_async_copy(ka_hbm, ka, local_sem.at[4]),
        pltpu.make_async_copy(w_hbm, weight.at[mine], local_sem.at[5]),
        pltpu.make_async_copy(va_hbm, va, local_sem.at[6]),
    ]
    for load in loads:
        load.start()

    barrier = pltpu.get_barrier_semaphore()
    for step in (1, -1):
        pl.semaphore_signal(barrier, inc=1, device_id={"blk": at_z(step), "head": head}, device_id_type=MESH)

    def greet(i, carry):
        to_blk, to_head = z * 4 + i % 4, i // 4

        @pl.when(jnp.logical_or(to_blk != blk, to_head != head))
        def _():
            pl.semaphore_signal(barrier, inc=1, device_id={"blk": to_blk, "head": to_head}, device_id_type=MESH)

        return carry

    lax.fori_loop(0, 32, greet, 0)
    pl.semaphore_wait(barrier, 33)

    key_sends = []

    def key_copy(slot, to_blk, to_head):
        copy = pltpu.make_async_remote_copy(
            src_ref=keys.at[slot],
            dst_ref=keys.at[slot],
            send_sem=key_send.at[len(key_sends)],
            recv_sem=key_recv.at[slot],
            device_id={"blk": to_blk, "head": to_head},
            device_id_type=MESH,
        )
        key_sends.append(copy)
        return copy

    def key_wait(slot):
        pltpu.make_async_remote_copy(
            src_ref=keys.at[slot],
            dst_ref=keys.at[slot],
            send_sem=key_send.at[0],
            recv_sem=key_recv.at[slot],
            device_id={"blk": sibling, "head": head},
            device_id_type=MESH,
        ).wait_recv()

    def w_copy(index, src, dst, to_blk, to_head):
        return pltpu.make_async_remote_copy(
            src_ref=src,
            dst_ref=dst,
            send_sem=w_send.at[index],
            recv_sem=w_recv.at[index],
            device_id={"blk": to_blk, "head": to_head},
            device_id_type=MESH,
        )

    carried = (yhi + x) % 2

    def carry_slot(step):
        return wrap_z(z + step) * 4 + carried * 2 + core

    def other_slot(step):
        return wrap_z(z + step) * 4 + (1 - carried) * 2 + core

    loads[0].wait()
    loads[1].wait()
    key_copy(blk, other_y, head_y).start()
    first = [key_copy(carry_slot(0), at_z(1), head), key_copy(carry_slot(0), at_z(-1), head)]

    @pl.when(x % 2 == 0)
    def _():
        for copy in first:
            copy.start()

    key_copy(blk, sibling, head).start()

    lane_max[...] = jnp.full_like(lane_max, -jnp.inf)

    for index in (2, 3, 4):
        loads[index].wait()
    for h in range(heads):
        product = jnp.dot(qn[:, h * nope:(h + 1) * nope], ka[h], preferred_element_type=F32)
        queries[h * rows:(h + 1) * rows, 0:lat] = product.astype(BF16)
        queries[h * rows:(h + 1) * rows, lat:lat + rope] = qr[:, h * rope:(h + 1) * rope]

    half = weight.shape[1] // 2
    own_w = weight.at[mine]
    far = flip(mine, 2)
    loads[5].wait()
    w_sends = [
        w_copy(0, weight.at[mine, pl.ds(0, half)], relay.at[0], other_y, head_y),
        w_copy(1, weight.at[mine, pl.ds(half, half)], relay.at[1], blk, head_y),
        w_copy(2, own_w, own_w, sibling, head),
    ]
    for copy in w_sends:
        copy.start()

    key_wait(flip(blk, 2))

    @pl.when(x % 2 == 1)
    def _():
        for copy in first:
            copy.start()

    key_copy(flip(blk, 2), sibling, head).start()

    def unit(step, half_y):
        base = wrap_z(z + step) * 4 + half_y * 2
        block = jnp.concatenate([keys[base], keys[base + 1]], axis=1)
        product = jnp.dot(queries[...], block, preferred_element_type=F32)
        scores[base // 2] = product
        width = block.shape[1] // 2
        lane_max[...] = jnp.maximum(lane_max[...], jnp.maximum(product[:, :width], product[:, width:]))

    def own_units(i, carry):
        half_y = (yhi + i) % 2
        key_wait(z * 4 + half_y * 2 + 1 - core)
        unit(0, half_y)
        return carry

    lax.fori_loop(0, 2, own_units, 0)

    def units(count, carry_step, other_step):
        def one(i, carry):
            late = i // 2
            step = (1 - 2 * (i % 2)) * (carry_step + (other_step - carry_step) * late)
            half_y = (carried + late) % 2
            key_wait(wrap_z(z + step) * 4 + half_y * 2 + 1 - core)
            unit(step, half_y)
            return carry

        lax.fori_loop(0, count, one, 0)

    for step in (1, 2, 3):
        for way in (1, -1):
            slot = carry_slot(-way * step)
            key_wait(slot)
            if step < 3:
                key_copy(slot, at_z(way), head).start()
            key_copy(slot, blk, at_x(way)).start()
            key_copy(slot, sibling, head).start()
        if step == 3:
            key_copy(carry_slot(-side * 3), at_z(side), head).start()
        if step > 1:
            for way in (1, -1):
                slot = other_slot(-way * (step - 1))
                key_wait(slot)
                key_copy(slot, sibling, head).start()
            units(2 if step == 2 else 4, step - 1, step - 2)
    slot = carry_slot(4)
    key_wait(slot)
    key_copy(slot, blk, at_x(side)).start()
    key_copy(slot, sibling, head).start()

    w_sends[0].wait_recv()
    w_sends[1].wait_recv()
    w_sends.append(w_copy(3, relay.at[0], weight.at[far, pl.ds(0, half)], blk, head_y))
    w_sends.append(w_copy(4, relay.at[1], weight.at[mine, pl.ds(half, half)], other_y, head_y))
    w_sends[3].start()
    w_sends[4].start()

    for way in (1, -1):
        slot = other_slot(-way * 3)
        key_wait(slot)
        key_copy(slot, sibling, head).start()
    units(4, 3, 2)
    slot = other_slot(4)
    key_wait(slot)
    key_copy(slot, sibling, head).start()

    def late_units(i, carry):
        is_far = i // 2
        step = (1 - 2 * (i % 2)) * 3 * (1 - is_far) + 4 * is_far
        half_y = (carried + (1 - is_far) + is_far * (i % 2)) % 2
        key_wait(wrap_z(z + step) * 4 + half_y * 2 + 1 - core)
        unit(step, half_y)
        return carry

    lax.fori_loop(0, 4, late_units, 0)

    att_sends = {}

    def att_copy(index, slot, group, to_blk):
        return pltpu.make_async_remote_copy(
            src_ref=att.at[slot, group],
            dst_ref=att.at[slot, group],
            send_sem=att_send.at[index],
            recv_sem=att_recv.at[slot, group],
            device_id={"blk": to_blk, "head": head},
            device_id_type=MESH,
        )

    def att_forward(step, group, way):
        copy = att_copy(len(att_sends), wrap_z(z - way * step), group, at_z(way))
        copy.start()
        att_sends[step, group, way] = copy

    def att_wait(slot, group):
        att_copy(0, slot, group, at_z(1)).wait_recv()

    def pass_on(step, group):
        for way in (1, -1):
            att_wait(wrap_z(z - way * step), group)
            if step < 3 or (group % 2 == 0) == (way == 1):
                att_forward(step, group, way)

    loads[6].wait()
    for group in range(GROUPS):
        rows_at = pl.ds(group * group_rows, group_rows)
        top = jnp.max(lane_max[rows_at], axis=1, keepdims=True)
        acc[...] = jnp.zeros_like(acc)
        lane_sum[...] = jnp.zeros_like(lane_sum)

        def mix(i, carry):
            value = jnp.concatenate([scores[2 * i, rows_at], scores[2 * i + 1, rows_at]], axis=1)
            value = jnp.exp2((value - top) * factor)
            width = lane_sum.shape[1]
            total = value[:, 0:width]
            for k in range(1, value.shape[1] // width):
                total = total + value[:, k * width:(k + 1) * width]
            lane_sum[...] += total
            block = jnp.concatenate([keys[4 * i + k, 0:lat] for k in range(4)], axis=1)
            acc[...] += lax.dot_general(
                value.astype(BF16), block, (((1,), (1,)), ((), ())), preferred_element_type=F32
            )
            return carry

        lax.fori_loop(0, scores.shape[0] // 2, mix, 0)
        row_sum = jnp.sum(lane_sum[...], axis=1, keepdims=True)
        mixture = (acc[...] / row_sum).astype(BF16)
        for h in range(group_heads):
            value = jnp.dot(mixture[h * rows:(h + 1) * rows], va[group * group_heads + h], preferred_element_type=F32)
            att[z, group, :, h * vd:(h + 1) * vd] = value.astype(BF16)
        for way in (1, -1):
            att_forward(0, group, way)
        if group > 0:
            pass_on(1, group - 1)
        if group == 2:
            w_sends[3].wait_recv()
            w_sends[4].wait_recv()
            w_sends.append(w_copy(5, weight.at[far], weight.at[far], sibling, head))
            w_sends[5].start()

    def out_copy(to_z, column):
        return pltpu.make_async_remote_copy(
            src_ref=part.at[to_z, column],
            dst_ref=summed.at[head * 4 + mine],
            send_sem=out_send.at[to_z * 4 + column],
            recv_sem=out_recv.at[head * 4 + mine],
            device_id={"blk": z * 4 + column, "head": to_z},
            device_id_type=MESH,
        )

    def project(slots):
        lhs = [jnp.concatenate([att[slot, group] for group in range(GROUPS)], axis=1) for slot in slots]
        lhs = jnp.concatenate(lhs, axis=0) if len(slots) > 1 else lhs[0]

        def one(column, carry):
            value = jnp.dot(lhs, weight[column], preferred_element_type=F32).astype(BF16)
            for k, slot in enumerate(slots):
                part[slot, column] = value[k * rows:(k + 1) * rows]
                here = jnp.logical_and(slot == head, column == mine)

                @pl.when(here)
                def _():
                    summed[head * 4 + mine] = value[k * rows:(k + 1) * rows]

                @pl.when(jnp.logical_not(here))
                def _():
                    out_copy(slot, column).start()

            return carry

        lax.fori_loop(0, 4, one, 0)

    pass_on(1, GROUPS - 1)
    w_sends[2].wait_recv()
    w_sends[5].wait_recv()
    project([z])
    for step in (2, 3):
        for group in range(GROUPS):
            pass_on(step, group)
            if group == 1:
                project([wrap_z(z - step + 1), wrap_z(z + step - 1)])
    project([wrap_z(z - 3), wrap_z(z + 3)])
    for group in range(GROUPS):
        att_wait(wrap_z(z + 4), group)
    project([wrap_z(z + 4)])

    def arrive(i, carry):
        @pl.when(i != head * 4 + mine)
        def _():
            pltpu.make_async_remote_copy(
                src_ref=part.at[0, 0],
                dst_ref=summed.at[i],
                send_sem=out_send.at[0],
                recv_sem=out_recv.at[i],
                device_id={"blk": sibling, "head": head},
                device_id_type=MESH,
            ).wait_recv()

        return carry

    lax.fori_loop(0, 32, arrive, 0)
    for k in range(4):
        total = summed[k].astype(F32)
        for h in range(1, 8):
            total = total + summed[4 * h + k].astype(F32)
        out_ref[k * rows:(k + 1) * rows] = total.astype(BF16)

    for copy in key_sends + w_sends + list(att_sends.values()):
        copy.wait_send()

    def leave(i, carry):
        to_z, column = i // 4, i % 4

        @pl.when(jnp.logical_or(to_z != head, column != mine))
        def _():
            out_copy(to_z, column).wait_send()

        return carry

    lax.fori_loop(0, 32, leave, 0)


def body(query_nope, query_rope, key_absorb, value_absorb, out_weight, latent_cache, rope_key):
    rows = query_nope.shape[0]
    heads, nope, lat = key_absorb.shape
    rope, docs = rope_key.shape
    vd = value_absorb.shape[2]
    depth, columns = out_weight.shape
    pairs = heads * rows
    group_rows = pairs // GROUPS
    any_spec = pl.BlockSpec(memory_space=pl.ANY)
    dma = pltpu.SemaphoreType.DMA
    return pl.pallas_call(
        kernel,
        out_shape=jax.ShapeDtypeStruct((4 * rows, columns), BF16),
        in_specs=[any_spec] * 7,
        out_specs=pl.BlockSpec(memory_space=pltpu.VMEM),
        scratch_shapes=[
            pltpu.VMEM((32, lat + rope, docs), BF16),
            pltpu.VMEM((pairs, lat + rope), BF16),
            pltpu.VMEM(query_nope.shape, BF16),
            pltpu.VMEM(query_rope.shape, BF16),
            pltpu.VMEM(key_absorb.shape, BF16),
            pltpu.VMEM(value_absorb.shape, BF16),
            pltpu.VMEM((4, depth, columns), BF16),
            pltpu.VMEM((2, depth // 2, columns), BF16),
            pltpu.VMEM((16, pairs, 2 * docs), F32),
            pltpu.VMEM((pairs, docs), F32),
            pltpu.VMEM((group_rows, docs), F32),
            pltpu.VMEM((group_rows, lat), F32),
            pltpu.VMEM((Z, GROUPS, rows, heads // GROUPS * vd), BF16),
            pltpu.VMEM((Z, 4, rows, columns), BF16),
            pltpu.VMEM((32, rows, columns), BF16),
            dma((7,)),
            dma((31,)),
            dma((32,)),
            dma((6,)),
            dma((6,)),
            dma((28,)),
            dma((Z, GROUPS)),
            dma((32,)),
            dma((32,)),
        ],
        compiler_params=pltpu.CompilerParams(
            collective_id=0, has_side_effects=True, vmem_limit_bytes=60 * 1024 * 1024
        ),
    )(query_nope, query_rope, key_absorb, value_absorb, out_weight, latent_cache, rope_key)


def solution(mesh):
    in_specs = (
        P("blk", "head"),
        P("blk", "head"),
        P("head", None, None),
        P("head", None, None),
        P("head", "blk"),
        P(None, "blk"),
        P(None, "blk"),
    )
    return jax.shard_map(body, mesh=mesh, in_specs=in_specs, out_specs=P("head", "blk"), check_vma=False)
```

```python
import functools
import math

import jax
import jax.numpy as jnp
from jax import lax
from jax.experimental import pallas as pl
from jax.experimental.pallas import tpu as pltpu
from jax.sharding import PartitionSpec as P

MESH = pl.DeviceIdType.MESH
F32 = jnp.float32
BF16 = jnp.bfloat16

Z = 8
X = 4
GROUPS = 4
PIECES = 4


def flip(value, bit):
    return value + bit - 2 * bit * (value // bit % 2)


def kernel(
    qn_hbm, qr_hbm, ka_hbm, va_hbm, w_hbm, lat_hbm, rk_hbm, out_ref,
    keys, keys_t, queries, qn, qr, ka, va, weight, scores, lane_max,
    att, part, summed,
    local_sem, key_send, key_recv, sib_send, sib_recv, w_send, w_recv, att_send, att_recv, out_send, out_recv,
):
    blk = lax.axis_index("blk")
    head = lax.axis_index("head")
    z = blk // 4
    mine = blk % 4
    yhi = mine // 2
    core = blk % 2
    x = head // 2
    sibling = flip(blk, 1)
    other_y = flip(blk, 2)
    head_y = flip(head, 1)
    side = 1 - 2 * core

    lat = lat_hbm.shape[0]
    rope = rk_hbm.shape[0]
    heads, nope = ka_hbm.shape[0], ka_hbm.shape[1]
    vd = va_hbm.shape[2]
    rows = qn_hbm.shape[0]
    group_heads = heads // GROUPS
    group_rows = group_heads * rows
    factor = (nope + rope) ** (-0.5) * math.log2(math.e)

    def wrap_z(value):
        return (value + 2 * Z) % Z

    def at_z(step):
        return wrap_z(z + step) * 4 + mine

    def at_x(step):
        return (x + step + X) % X * 2 + head % 2

    barrier = pltpu.get_barrier_semaphore()
    for step in (1, -1):
        pl.semaphore_signal(barrier, inc=1, device_id={"blk": at_z(step), "head": head}, device_id_type=MESH)

    def greet(i, carry):
        to_blk, to_head = z * 4 + i % 4, i // 4

        @pl.when(jnp.logical_or(to_blk != blk, to_head != head))
        def _():
            pl.semaphore_signal(barrier, inc=1, device_id={"blk": to_blk, "head": to_head}, device_id_type=MESH)

        return carry

    lax.fori_loop(0, 32, greet, 0)
    loads = [
        pltpu.make_async_copy(lat_hbm, keys.at[blk, pl.ds(0, lat)], local_sem.at[0]),
        pltpu.make_async_copy(rk_hbm, keys.at[blk, pl.ds(lat, rope)], local_sem.at[1]),
        pltpu.make_async_copy(qn_hbm, qn, local_sem.at[2]),
        pltpu.make_async_copy(qr_hbm, qr, local_sem.at[3]),
        pltpu.make_async_copy(ka_hbm, ka, local_sem.at[4]),
        pltpu.make_async_copy(w_hbm, weight.at[mine], local_sem.at[5]),
        pltpu.make_async_copy(va_hbm, va, local_sem.at[6]),
    ]
    for load in loads:
        load.start()

    pl.semaphore_wait(barrier, 33)

    depth = (lat + rope) // PIECES
    sends = []
    whole = []

    def piece_copy(index, slot, p, to_blk, to_head):
        at = keys.at[slot, pl.ds(pl.multiple_of(p * depth, 16), depth)]
        return pltpu.make_async_remote_copy(
            src_ref=at,
            dst_ref=at,
            send_sem=key_send.at[index, p],
            recv_sem=key_recv.at[slot, p],
            device_id={"blk": to_blk, "head": to_head},
            device_id_type=MESH,
        )

    def new_send():
        sends.append(None)
        return len(sends) - 1

    def piece_wait(slot, p):
        piece_copy(0, slot, p, sibling, head).wait_recv()

    def pieces_wait(slot):
        def one(p, carry):
            piece_wait(slot, p)
            return carry

        lax.fori_loop(0, PIECES, one, 0)

    def send_pieces(*targets):
        def one(p, carry):
            for index, slot, to_blk, to_head in targets:
                piece_copy(index, slot, p, to_blk, to_head).start()
            return carry

        lax.fori_loop(0, PIECES, one, 0)

    def sib_copy(index, slot):
        return pltpu.make_async_remote_copy(
            src_ref=keys.at[slot],
            dst_ref=keys.at[slot],
            send_sem=sib_send.at[index],
            recv_sem=sib_recv.at[slot],
            device_id={"blk": sibling, "head": head},
            device_id_type=MESH,
        )

    def to_sibling(slot):
        copy = sib_copy(len(whole), slot)
        copy.start()
        whole.append(copy)

    def w_copy(index, src, dst, to_blk):
        return pltpu.make_async_remote_copy(
            src_ref=src,
            dst_ref=dst,
            send_sem=w_send.at[index],
            recv_sem=w_recv.at[index],
            device_id={"blk": to_blk, "head": head},
            device_id_type=MESH,
        )

    carried = (yhi + x) % 2

    def carry_slot(step):
        return wrap_z(z + step) * 4 + carried * 2 + core

    def other_slot(step):
        return wrap_z(z + step) * 4 + (1 - carried) * 2 + core

    loads[0].wait()
    loads[1].wait()
    across, up, down = new_send(), new_send(), new_send()
    send_pieces((across, blk, other_y, head_y))

    @pl.when(x % 2 == 0)
    def _():
        send_pieces((up, blk, at_z(1), head), (down, blk, at_z(-1), head))

    to_sibling(blk)

    lane_max[...] = jnp.full_like(lane_max, -jnp.inf)

    for index in (2, 3, 4):
        loads[index].wait()
    for h in range(heads):
        product = jnp.dot(qn[:, h * nope:(h + 1) * nope], ka[h], preferred_element_type=F32)
        queries[h * rows:(h + 1) * rows, 0:lat] = product.astype(BF16)
        queries[h * rows:(h + 1) * rows, lat:lat + rope] = qr[:, h * rope:(h + 1) * rope]

    def across_piece(p, carry):
        piece_wait(flip(blk, 2), p)

        @pl.when(x % 2 == 1)
        def _():
            piece_copy(up, flip(blk, 2), p, at_z(1), head).start()
            piece_copy(down, flip(blk, 2), p, at_z(-1), head).start()

        return carry

    lax.fori_loop(0, PIECES, across_piece, 0)
    to_sibling(flip(blk, 2))

    own_w = weight.at[mine]
    far = flip(mine, 2)
    loads[5].wait()
    w_sends = [w_copy(0, own_w, own_w, other_y), w_copy(1, own_w, own_w, sibling)]
    for copy in w_sends:
        copy.start()

    def unit(step, half_y):
        base = wrap_z(z + step) * 4 + half_y * 2
        sib_copy(0, base + 1 - core).wait_recv()
        block = jnp.concatenate([keys[base], keys[base + 1]], axis=1)
        product = jnp.dot(queries[...], block, preferred_element_type=F32)
        scores[base // 2] = product
        keys_t[base // 2] = block[0:lat].T
        width = block.shape[1] // 2
        lane_max[...] = jnp.maximum(lane_max[...], jnp.maximum(product[:, :width], product[:, width:]))

    def units(i, carry_step, other_step):
        late = i // 2
        step = (1 - 2 * (i % 2)) * (carry_step + (other_step - carry_step) * late)
        unit(step, (carried + late) % 2)

    def advance(step):
        ways = (1, -1)
        forward = [new_send() for _ in ways] if step < 3 else [new_send()]
        along_x = [new_send() for _ in ways]

        def one(p, carry):
            for k, way in enumerate(ways):
                slot = carry_slot(-way * step)
                piece_wait(slot, p)
                if step < 3:
                    piece_copy(forward[k], slot, p, at_z(way), head).start()
            if step == 3:
                piece_copy(forward[0], carry_slot(-side * 3), p, at_z(side), head).start()
            for k, way in enumerate(ways):
                piece_copy(along_x[k], carry_slot(-way * step), p, blk, at_x(way)).start()
            if step == 3:
                units(p, 2, 1)
            else:
                @pl.when(p % 2 == 1)
                def _():
                    if step == 1:
                        unit(0, (yhi + p // 2) % 2)
                    else:
                        unit(1 - 2 * (p // 2), carried)

            return carry

        lax.fori_loop(0, PIECES, one, 0)
        for way in ways:
            to_sibling(carry_slot(-way * step))
        if step > 1:
            for way in ways:
                pieces_wait(other_slot(-way * (step - 1)))
                to_sibling(other_slot(-way * (step - 1)))

    for step in (1, 2, 3):
        advance(step)
    last = new_send()

    def last_piece(p, carry):
        piece_wait(carry_slot(4), p)
        piece_copy(last, carry_slot(4), p, blk, at_x(side)).start()
        units(p, 3, 2)
        return carry

    lax.fori_loop(0, PIECES, last_piece, 0)
    to_sibling(carry_slot(4))
    for way in (1, -1):
        pieces_wait(other_slot(-way * 3))
        to_sibling(other_slot(-way * 3))
    pieces_wait(other_slot(4))
    to_sibling(other_slot(4))

    def tail_units(i, carry):
        middle = (i + 1) // 2 % 2
        step = 4 * (1 - middle) + middle * 3 * (3 - 2 * i)
        unit(step, (carried + (i + 2) // 3) % 2)
        return carry

    lax.fori_loop(0, 4, tail_units, 0)

    att_sends = {}

    def att_copy(index, slot, group, to_blk):
        return pltpu.make_async_remote_copy(
            src_ref=att.at[slot, group],
            dst_ref=att.at[slot, group],
            send_sem=att_send.at[index],
            recv_sem=att_recv.at[slot, group],
            device_id={"blk": to_blk, "head": head},
            device_id_type=MESH,
        )

    def att_forward(step, group, way):
        copy = att_copy(len(att_sends), wrap_z(z - way * step), group, at_z(way))
        copy.start()
        att_sends[step, group, way] = copy

    def att_wait(slot, group):
        att_copy(0, slot, group, at_z(1)).wait_recv()

    def pass_on(step, group):
        for way in (1, -1):
            att_wait(wrap_z(z - way * step), group)
            if step < 3 or (group % 2 == 0) == (way == 1):
                att_forward(step, group, way)

    loads[6].wait()
    for group in range(GROUPS):
        rows_at = pl.ds(group * group_rows, group_rows)
        top = jnp.max(lane_max[rows_at], axis=1, keepdims=True)
        count = scores.shape[0]
        weights, total = [], None
        for u in range(count):
            value = jnp.exp2((scores[u, rows_at] - top) * factor)
            weights.append(value.astype(BF16))
            width = value.shape[1] // 2
            value = value[:, :width] + value[:, width:]
            total = value if total is None else total + value
        mixed = jnp.dot(
            jnp.concatenate(weights, axis=1), keys_t[...].reshape(-1, lat), preferred_element_type=F32
        )
        mixture = (mixed / jnp.sum(total, axis=1, keepdims=True)).astype(BF16)
        for h in range(group_heads):
            value = jnp.dot(mixture[h * rows:(h + 1) * rows], va[group * group_heads + h], preferred_element_type=F32)
            att[z, group, :, h * vd:(h + 1) * vd] = value.astype(BF16)
        for way in (1, -1):
            att_forward(0, group, way)
        if group == 2:
            w_sends[0].wait_recv()
            w_sends.append(w_copy(2, weight.at[far], weight.at[far], sibling))
            w_sends[2].start()

    def out_copy(to_z, column):
        return pltpu.make_async_remote_copy(
            src_ref=part.at[to_z, column],
            dst_ref=summed.at[head * 4 + mine],
            send_sem=out_send.at[to_z * 4 + column],
            recv_sem=out_recv.at[head * 4 + mine],
            device_id={"blk": z * 4 + column, "head": to_z},
            device_id_type=MESH,
        )

    def project(slots):
        lhs = [jnp.concatenate([att[slot, group] for group in range(GROUPS)], axis=1) for slot in slots]
        lhs = jnp.concatenate(lhs, axis=0) if len(slots) > 1 else lhs[0]

        def one(column, carry):
            value = lax.dot_general(
                lhs, weight[column], (((1,), (1,)), ((), ())), preferred_element_type=F32
            ).astype(BF16)
            for k, slot in enumerate(slots):
                part[slot, column] = value[k * rows:(k + 1) * rows]
                here = jnp.logical_and(slot == head, column == mine)

                @pl.when(here)
                def _():
                    summed[head * 4 + mine] = value[k * rows:(k + 1) * rows]

                @pl.when(jnp.logical_not(here))
                def _():
                    out_copy(slot, column).start()

            return carry

        lax.fori_loop(0, 4, one, 0)

    for group in range(GROUPS):
        pass_on(1, group)
    w_sends[1].wait_recv()
    w_sends[2].wait_recv()
    project([z])
    for step in (2, 3):
        for group in range(GROUPS):
            pass_on(step, group)
            if group == 1:
                project([wrap_z(z - step + 1), wrap_z(z + step - 1)])
    project([wrap_z(z - 3), wrap_z(z + 3)])
    for group in range(GROUPS):
        att_wait(wrap_z(z + 4), group)
    project([wrap_z(z + 4)])

    def arrive(i, carry):
        @pl.when(i != head * 4 + mine)
        def _():
            pltpu.make_async_remote_copy(
                src_ref=part.at[0, 0],
                dst_ref=summed.at[i],
                send_sem=out_send.at[0],
                recv_sem=out_recv.at[i],
                device_id={"blk": sibling, "head": head},
                device_id_type=MESH,
            ).wait_recv()

        return carry

    lax.fori_loop(0, 32, arrive, 0)
    totals = []
    for k in range(4):
        total = summed[k].astype(F32)
        for h in range(1, 8):
            total = total + summed[4 * h + k].astype(F32)
        totals.append(total)

    out_ref[...] = jnp.concatenate(totals, axis=0).T.astype(BF16)

    def left(i, carry):
        piece_copy(i // PIECES, blk, i % PIECES, sibling, head).wait_send()
        return carry

    lax.fori_loop(0, len(sends) * PIECES, left, 0)
    for copy in whole + w_sends + list(att_sends.values()):
        copy.wait_send()

    def leave(i, carry):
        to_z, column = i // 4, i % 4

        @pl.when(jnp.logical_or(to_z != head, column != mine))
        def _():
            out_copy(to_z, column).wait_send()

        return carry

    lax.fori_loop(0, 32, leave, 0)


def body(query_nope, query_rope, key_absorb, value_absorb, out_weight, latent_cache, rope_key):
    out_weight = out_weight.T
    rows = query_nope.shape[0]
    heads, nope, lat = key_absorb.shape
    rope, docs = rope_key.shape
    vd = value_absorb.shape[2]
    columns, depth = out_weight.shape
    pairs = heads * rows
    any_spec = pl.BlockSpec(memory_space=pl.ANY)
    dma = pltpu.SemaphoreType.DMA
    return pl.pallas_call(
        kernel,
        out_shape=jax.ShapeDtypeStruct((columns, 4 * rows), BF16),
        in_specs=[any_spec] * 7,
        out_specs=pl.BlockSpec(memory_space=pltpu.VMEM),
        scratch_shapes=[
            pltpu.VMEM((32, lat + rope, docs), BF16),
            pltpu.VMEM((16, 2 * docs, lat), BF16),
            pltpu.VMEM((pairs, lat + rope), BF16),
            pltpu.VMEM(query_nope.shape, BF16),
            pltpu.VMEM(query_rope.shape, BF16),
            pltpu.VMEM(key_absorb.shape, BF16),
            pltpu.VMEM(value_absorb.shape, BF16),
            pltpu.VMEM((4, columns, depth), BF16),
            pltpu.VMEM((16, pairs, 2 * docs), F32),
            pltpu.VMEM((pairs, docs), F32),
            pltpu.VMEM((Z, GROUPS, rows, heads // GROUPS * vd), BF16),
            pltpu.VMEM((Z, 4, rows, columns), BF16),
            pltpu.VMEM((32, rows, columns), BF16),
            dma((7,)),
            dma((15, PIECES)),
            dma((32, PIECES)),
            dma((16,)),
            dma((32,)),
            dma((3,)),
            dma((3,)),
            dma((28,)),
            dma((Z, GROUPS)),
            dma((32,)),
            dma((32,)),
        ],
        compiler_params=pltpu.CompilerParams(
            collective_id=0, has_side_effects=True, vmem_limit_bytes=60 * 1024 * 1024
        ),
    )(query_nope, query_rope, key_absorb, value_absorb, out_weight, latent_cache, rope_key).T


def solution(mesh):
    in_specs = (
        P("blk", "head"),
        P("blk", "head"),
        P("head", None, None),
        P("head", None, None),
        P("head", "blk"),
        P(None, "blk"),
        P(None, "blk"),
    )
    return jax.shard_map(body, mesh=mesh, in_specs=in_specs, out_specs=P("head", "blk"), check_vma=False)
```

```python
import functools
import math

import jax
import jax.numpy as jnp
from jax import lax
from jax.experimental import pallas as pl
from jax.experimental.pallas import tpu as pltpu
from jax.sharding import PartitionSpec as P

MESH = pl.DeviceIdType.MESH
F32 = jnp.float32
BF16 = jnp.bfloat16

Z = 8
X = 4
GROUPS = 4
PIECES = 4


def flip(value, bit):
    return value + bit - 2 * bit * (value // bit % 2)


def kernel(
    qn_hbm, qr_hbm, ka_hbm, va_hbm, w_hbm, lat_hbm, rk_hbm, out_ref,
    keys, keys_t, queries, qn, qr, ka, va, weight, scores, lane_max,
    att, part, summed,
    local_sem, key_send, key_recv, sib_send, sib_recv, w_send, w_recv, att_send, att_recv, out_send, out_recv,
):
    blk = lax.axis_index("blk")
    head = lax.axis_index("head")
    z = blk // 4
    mine = blk % 4
    yhi = mine // 2
    core = blk % 2
    x = head // 2
    sibling = flip(blk, 1)
    other_y = flip(blk, 2)
    head_y = flip(head, 1)
    side = 1 - 2 * core

    lat = lat_hbm.shape[0]
    rope = rk_hbm.shape[0]
    heads, nope = ka_hbm.shape[0], ka_hbm.shape[1]
    vd = va_hbm.shape[2]
    rows = qn_hbm.shape[0]
    group_heads = heads // GROUPS
    group_rows = group_heads * rows
    factor = (nope + rope) ** (-0.5) * math.log2(math.e)

    def wrap_z(value):
        return (value + 2 * Z) % Z

    def at_z(step):
        return wrap_z(z + step) * 4 + mine

    def at_x(step):
        return (x + step + X) % X * 2 + head % 2

    barrier = pltpu.get_barrier_semaphore()
    for step in (1, -1):
        pl.semaphore_signal(barrier, inc=1, device_id={"blk": at_z(step), "head": head}, device_id_type=MESH)

    for to_blk, to_head in ((blk, at_x(1)), (blk, at_x(-1)), (other_y, head_y), (other_y, head), (sibling, head)):
        pl.semaphore_signal(barrier, inc=1, device_id={"blk": to_blk, "head": to_head}, device_id_type=MESH)

    loads = [
        pltpu.make_async_copy(lat_hbm, keys.at[blk, pl.ds(0, lat)], local_sem.at[0]),
        pltpu.make_async_copy(rk_hbm, keys.at[blk, pl.ds(lat, rope)], local_sem.at[1]),
        pltpu.make_async_copy(qn_hbm, qn, local_sem.at[2]),
        pltpu.make_async_copy(qr_hbm, qr, local_sem.at[3]),
        pltpu.make_async_copy(ka_hbm, ka, local_sem.at[4]),
        pltpu.make_async_copy(w_hbm, weight.at[mine], local_sem.at[5]),
        pltpu.make_async_copy(va_hbm, va, local_sem.at[6]),
    ]
    for load in loads:
        load.start()

    pl.semaphore_wait(barrier, 7)

    depth = (lat + rope) // PIECES
    sends = []
    whole = []

    def piece_copy(index, slot, p, to_blk, to_head):
        at = keys.at[slot, pl.ds(pl.multiple_of(p * depth, 16), depth)]
        return pltpu.make_async_remote_copy(
            src_ref=at,
            dst_ref=at,
            send_sem=key_send.at[index, p],
            recv_sem=key_recv.at[slot, p],
            device_id={"blk": to_blk, "head": to_head},
            device_id_type=MESH,
        )

    def new_send():
        sends.append(None)
        return len(sends) - 1

    def piece_wait(slot, p):
        piece_copy(0, slot, p, sibling, head).wait_recv()

    def pieces_wait(slot):
        def one(p, carry):
            piece_wait(slot, p)
            return carry

        lax.fori_loop(0, PIECES, one, 0)

    def send_pieces(*targets):
        def one(p, carry):
            for index, slot, to_blk, to_head in targets:
                piece_copy(index, slot, p, to_blk, to_head).start()
            return carry

        lax.fori_loop(0, PIECES, one, 0)

    def sib_copy(index, slot):
        return pltpu.make_async_remote_copy(
            src_ref=keys.at[slot],
            dst_ref=keys.at[slot],
            send_sem=sib_send.at[index],
            recv_sem=sib_recv.at[slot],
            device_id={"blk": sibling, "head": head},
            device_id_type=MESH,
        )

    def to_sibling(slot):
        copy = sib_copy(len(whole), slot)
        copy.start()
        whole.append(copy)

    def w_copy(index, src, dst, to_blk):
        return pltpu.make_async_remote_copy(
            src_ref=src,
            dst_ref=dst,
            send_sem=w_send.at[index],
            recv_sem=w_recv.at[index],
            device_id={"blk": to_blk, "head": head},
            device_id_type=MESH,
        )

    carried = (yhi + x) % 2

    def carry_slot(step):
        return wrap_z(z + step) * 4 + carried * 2 + core

    def other_slot(step):
        return wrap_z(z + step) * 4 + (1 - carried) * 2 + core

    loads[0].wait()
    loads[1].wait()
    across, up, down = new_send(), new_send(), new_send()
    send_pieces((across, blk, other_y, head_y))

    @pl.when(x % 2 == 0)
    def _():
        send_pieces((up, blk, at_z(1), head), (down, blk, at_z(-1), head))

    to_sibling(blk)

    lane_max[...] = jnp.full_like(lane_max, -jnp.inf)

    for index in (2, 3, 4):
        loads[index].wait()
    for h in range(heads):
        product = jnp.dot(qn[:, h * nope:(h + 1) * nope], ka[h], preferred_element_type=F32)
        queries[h * rows:(h + 1) * rows, 0:lat] = product.astype(BF16)
        queries[h * rows:(h + 1) * rows, lat:lat + rope] = qr[:, h * rope:(h + 1) * rope]

    def across_piece(p, carry):
        piece_wait(flip(blk, 2), p)

        @pl.when(x % 2 == 1)
        def _():
            piece_copy(up, flip(blk, 2), p, at_z(1), head).start()
            piece_copy(down, flip(blk, 2), p, at_z(-1), head).start()

        return carry

    lax.fori_loop(0, PIECES, across_piece, 0)
    to_sibling(flip(blk, 2))

    own_w = weight.at[mine]
    far = flip(mine, 2)
    loads[5].wait()
    w_sends = [w_copy(0, own_w, own_w, other_y), w_copy(1, own_w, own_w, sibling)]
    for copy in w_sends:
        copy.start()

    def unit(step, half_y):
        base = wrap_z(z + step) * 4 + half_y * 2
        sib_copy(0, base + 1 - core).wait_recv()
        block = jnp.concatenate([keys[base], keys[base + 1]], axis=1)
        product = jnp.dot(queries[...], block, preferred_element_type=F32)
        scores[base // 2] = product
        keys_t[base // 2] = block[0:lat].T
        width = block.shape[1] // 2
        lane_max[...] = jnp.maximum(lane_max[...], jnp.maximum(product[:, :width], product[:, width:]))

    def units(i, carry_step, other_step):
        late = i // 2
        step = (1 - 2 * (i % 2)) * (carry_step + (other_step - carry_step) * late)
        unit(step, (carried + late) % 2)

    def advance(step):
        ways = (1, -1)
        forward = [new_send() for _ in ways] if step < 3 else [new_send()]
        along_x = [new_send() for _ in ways]

        def one(p, carry):
            for k, way in enumerate(ways):
                slot = carry_slot(-way * step)
                piece_wait(slot, p)
                if step < 3:
                    piece_copy(forward[k], slot, p, at_z(way), head).start()
            if step == 3:
                piece_copy(forward[0], carry_slot(-side * 3), p, at_z(side), head).start()
            for k, way in enumerate(ways):
                piece_copy(along_x[k], carry_slot(-way * step), p, blk, at_x(way)).start()
            if step == 3:
                units(p, 2, 1)
            else:
                @pl.when(p % 2 == 1)
                def _():
                    if step == 1:
                        unit(0, (yhi + p // 2) % 2)
                    else:
                        unit(1 - 2 * (p // 2), carried)

            return carry

        lax.fori_loop(0, PIECES, one, 0)
        for way in ways:
            to_sibling(carry_slot(-way * step))
        if step > 1:
            for way in ways:
                pieces_wait(other_slot(-way * (step - 1)))
                to_sibling(other_slot(-way * (step - 1)))

    for step in (1, 2, 3):
        advance(step)
    last = new_send()

    def last_piece(p, carry):
        piece_wait(carry_slot(4), p)
        piece_copy(last, carry_slot(4), p, blk, at_x(side)).start()
        units(p, 3, 2)
        return carry

    lax.fori_loop(0, PIECES, last_piece, 0)
    to_sibling(carry_slot(4))
    for way in (1, -1):
        pieces_wait(other_slot(-way * 3))
        to_sibling(other_slot(-way * 3))
    pieces_wait(other_slot(4))
    to_sibling(other_slot(4))

    def tail_units(i, carry):
        middle = (i + 1) // 2 % 2
        step = 4 * (1 - middle) + middle * 3 * (3 - 2 * i)
        unit(step, (carried + (i + 2) // 3) % 2)
        return carry

    lax.fori_loop(0, 4, tail_units, 0)

    att_sends = {}

    def att_copy(index, slot, group, to_blk):
        return pltpu.make_async_remote_copy(
            src_ref=att.at[slot, group],
            dst_ref=att.at[slot, group],
            send_sem=att_send.at[index],
            recv_sem=att_recv.at[slot, group],
            device_id={"blk": to_blk, "head": head},
            device_id_type=MESH,
        )

    def att_forward(step, group, way):
        copy = att_copy(len(att_sends), wrap_z(z - way * step), group, at_z(way))
        copy.start()
        att_sends[step, group, way] = copy

    def att_wait(slot, group):
        att_copy(0, slot, group, at_z(1)).wait_recv()

    def pass_on(step, group):
        for way in (1, -1):
            att_wait(wrap_z(z - way * step), group)
            if step < 3 or (group % 2 == 0) == (way == 1):
                att_forward(step, group, way)

    loads[6].wait()
    for group in range(GROUPS):
        rows_at = pl.ds(group * group_rows, group_rows)
        top = jnp.max(lane_max[rows_at], axis=1, keepdims=True)
        count = scores.shape[0]
        weights, total = [], None
        for u in range(count):
            value = jnp.exp2((scores[u, rows_at] - top) * factor)
            weights.append(value.astype(BF16))
            width = value.shape[1] // 2
            value = value[:, :width] + value[:, width:]
            total = value if total is None else total + value
        mixed = jnp.dot(
            jnp.concatenate(weights, axis=1), keys_t[...].reshape(-1, lat), preferred_element_type=F32
        )
        mixture = (mixed / jnp.sum(total, axis=1, keepdims=True)).astype(BF16)
        for h in range(group_heads):
            value = jnp.dot(mixture[h * rows:(h + 1) * rows], va[group * group_heads + h], preferred_element_type=F32)
            att[z, group, :, h * vd:(h + 1) * vd] = value.astype(BF16)
        for way in (1, -1):
            att_forward(0, group, way)
        if group == 2:
            w_sends[0].wait_recv()
            w_sends.append(w_copy(2, weight.at[far], weight.at[far], sibling))
            w_sends[2].start()

    def out_copy(to_z, column):
        return pltpu.make_async_remote_copy(
            src_ref=part.at[to_z, column],
            dst_ref=summed.at[head * 4 + mine],
            send_sem=out_send.at[to_z * 4 + column],
            recv_sem=out_recv.at[head * 4 + mine],
            device_id={"blk": z * 4 + column, "head": to_z},
            device_id_type=MESH,
        )

    def project(slots):
        lhs = [jnp.concatenate([att[slot, group] for group in range(GROUPS)], axis=1) for slot in slots]
        lhs = jnp.concatenate(lhs, axis=0) if len(slots) > 1 else lhs[0]

        def one(column, carry):
            value = lax.dot_general(
                lhs, weight[column], (((1,), (1,)), ((), ())), preferred_element_type=F32
            ).astype(BF16)
            for k, slot in enumerate(slots):
                part[slot, column] = value[k * rows:(k + 1) * rows]
                here = jnp.logical_and(slot == head, column == mine)

                @pl.when(here)
                def _():
                    summed[head * 4 + mine] = value[k * rows:(k + 1) * rows]

                @pl.when(jnp.logical_not(here))
                def _():
                    out_copy(slot, column).start()

            return carry

        lax.fori_loop(0, 4, one, 0)

    pass_on(1, 0)
    w_sends[1].wait_recv()
    w_sends[2].wait_recv()
    project([z])
    for group in range(1, GROUPS):
        pass_on(1, group)
    project([wrap_z(z - 1), wrap_z(z + 1)])
    for step in (2, 3):
        for group in range(GROUPS):
            pass_on(step, group)
        project([wrap_z(z - step), wrap_z(z + step)])
    for group in range(GROUPS):
        att_wait(wrap_z(z + 4), group)
    project([wrap_z(z + 4)])

    def arrive(i, carry):
        @pl.when(i != head * 4 + mine)
        def _():
            pltpu.make_async_remote_copy(
                src_ref=part.at[0, 0],
                dst_ref=summed.at[i],
                send_sem=out_send.at[0],
                recv_sem=out_recv.at[i],
                device_id={"blk": sibling, "head": head},
                device_id_type=MESH,
            ).wait_recv()

        return carry

    lax.fori_loop(0, 32, arrive, 0)
    totals = []
    for k in range(4):
        total = summed[k].astype(F32)
        for h in range(1, 8):
            total = total + summed[4 * h + k].astype(F32)
        totals.append(total)

    out_ref[...] = jnp.concatenate(totals, axis=0).T.astype(BF16)

    def left(i, carry):
        piece_copy(i // PIECES, blk, i % PIECES, sibling, head).wait_send()
        return carry

    lax.fori_loop(0, len(sends) * PIECES, left, 0)
    for copy in whole + w_sends + list(att_sends.values()):
        copy.wait_send()

    def leave(i, carry):
        to_z, column = i // 4, i % 4

        @pl.when(jnp.logical_or(to_z != head, column != mine))
        def _():
            out_copy(to_z, column).wait_send()

        return carry

    lax.fori_loop(0, 32, leave, 0)


def body(query_nope, query_rope, key_absorb, value_absorb, out_weight, latent_cache, rope_key):
    out_weight = out_weight.T
    rows = query_nope.shape[0]
    heads, nope, lat = key_absorb.shape
    rope, docs = rope_key.shape
    vd = value_absorb.shape[2]
    columns, depth = out_weight.shape
    pairs = heads * rows
    any_spec = pl.BlockSpec(memory_space=pl.ANY)
    dma = pltpu.SemaphoreType.DMA
    return pl.pallas_call(
        kernel,
        out_shape=jax.ShapeDtypeStruct((columns, 4 * rows), BF16),
        in_specs=[any_spec] * 7,
        out_specs=pl.BlockSpec(memory_space=pltpu.VMEM),
        scratch_shapes=[
            pltpu.VMEM((32, lat + rope, docs), BF16),
            pltpu.VMEM((16, 2 * docs, lat), BF16),
            pltpu.VMEM((pairs, lat + rope), BF16),
            pltpu.VMEM(query_nope.shape, BF16),
            pltpu.VMEM(query_rope.shape, BF16),
            pltpu.VMEM(key_absorb.shape, BF16),
            pltpu.VMEM(value_absorb.shape, BF16),
            pltpu.VMEM((4, columns, depth), BF16),
            pltpu.VMEM((16, pairs, 2 * docs), F32),
            pltpu.VMEM((pairs, docs), F32),
            pltpu.VMEM((Z, GROUPS, rows, heads // GROUPS * vd), BF16),
            pltpu.VMEM((Z, 4, rows, columns), BF16),
            pltpu.VMEM((32, rows, columns), BF16),
            dma((7,)),
            dma((15, PIECES)),
            dma((32, PIECES)),
            dma((16,)),
            dma((32,)),
            dma((3,)),
            dma((3,)),
            dma((28,)),
            dma((Z, GROUPS)),
            dma((32,)),
            dma((32,)),
        ],
        compiler_params=pltpu.CompilerParams(
            collective_id=0, has_side_effects=True, vmem_limit_bytes=60 * 1024 * 1024
        ),
    )(query_nope, query_rope, key_absorb, value_absorb, out_weight, latent_cache, rope_key).T


def solution(mesh):
    in_specs = (
        P("blk", "head"),
        P("blk", "head"),
        P("head", None, None),
        P("head", None, None),
        P("head", "blk"),
        P(None, "blk"),
        P(None, "blk"),
    )
    return jax.shard_map(body, mesh=mesh, in_specs=in_specs, out_specs=P("head", "blk"), check_vma=False)
```

```python
import functools
import math

import jax
import jax.numpy as jnp
from jax import lax
from jax.experimental import pallas as pl
from jax.experimental.pallas import tpu as pltpu
from jax.sharding import PartitionSpec as P

MESH = pl.DeviceIdType.MESH
F32 = jnp.float32
BF16 = jnp.bfloat16

Z = 8
X = 4
GROUPS = 4
PIECES = 4


def flip(value, bit):
    return value + bit - 2 * bit * (value // bit % 2)


def kernel(
    qn_hbm, qr_hbm, ka_hbm, va_hbm, w_hbm, lat_hbm, rk_hbm, out_ref,
    keys, keys_t, queries, qn, qr, ka, va, weight, scores, lane_max, top, lane_sum, acc,
    att, part, summed, totals,
    local_sem, key_send, key_recv, sib_send, sib_recv, w_send, w_recv, att_send, att_recv, out_send, out_recv,
):
    blk = lax.axis_index("blk")
    head = lax.axis_index("head")
    z = blk // 4
    mine = blk % 4
    yhi = mine // 2
    core = blk % 2
    x = head // 2
    sibling = flip(blk, 1)
    other_y = flip(blk, 2)
    head_y = flip(head, 1)
    side = 1 - 2 * core

    lat = lat_hbm.shape[0]
    rope = rk_hbm.shape[0]
    heads, nope = ka_hbm.shape[0], ka_hbm.shape[1]
    vd = va_hbm.shape[2]
    rows = qn_hbm.shape[0]
    group_heads = heads // GROUPS
    group_rows = group_heads * rows
    factor = (nope + rope) ** (-0.5) * math.log2(math.e)

    def wrap_z(value):
        return (value + 2 * Z) % Z

    def at_z(step):
        return wrap_z(z + step) * 4 + mine

    def at_x(step):
        return (x + step + X) % X * 2 + head % 2

    barrier = pltpu.get_barrier_semaphore()
    for step in (1, -1):
        pl.semaphore_signal(barrier, inc=1, device_id={"blk": at_z(step), "head": head}, device_id_type=MESH)

    for to_blk, to_head in ((blk, at_x(1)), (blk, at_x(-1)), (other_y, head_y), (other_y, head), (sibling, head)):
        pl.semaphore_signal(barrier, inc=1, device_id={"blk": to_blk, "head": to_head}, device_id_type=MESH)

    loads = [
        pltpu.make_async_copy(lat_hbm, keys.at[blk, pl.ds(0, lat)], local_sem.at[0]),
        pltpu.make_async_copy(rk_hbm, keys.at[blk, pl.ds(lat, rope)], local_sem.at[1]),
        pltpu.make_async_copy(qn_hbm, qn, local_sem.at[2]),
        pltpu.make_async_copy(qr_hbm, qr, local_sem.at[3]),
        pltpu.make_async_copy(ka_hbm, ka, local_sem.at[4]),
        pltpu.make_async_copy(w_hbm, weight.at[mine], local_sem.at[5]),
        pltpu.make_async_copy(va_hbm, va, local_sem.at[6]),
    ]
    for load in loads:
        load.start()

    pl.semaphore_wait(barrier, 7)

    depth = (lat + rope) // PIECES
    sends = []
    whole = []

    def piece_copy(index, slot, p, to_blk, to_head):
        at = keys.at[slot, pl.ds(pl.multiple_of(p * depth, 16), depth)]
        return pltpu.make_async_remote_copy(
            src_ref=at,
            dst_ref=at,
            send_sem=key_send.at[index, p],
            recv_sem=key_recv.at[slot, p],
            device_id={"blk": to_blk, "head": to_head},
            device_id_type=MESH,
        )

    def new_send():
        sends.append(None)
        return len(sends) - 1

    def piece_wait(slot, p):
        piece_copy(0, slot, p, sibling, head).wait_recv()

    def pieces_wait(slot):
        def one(p, carry):
            piece_wait(slot, p)
            return carry

        lax.fori_loop(0, PIECES, one, 0)

    def send_pieces(*targets):
        def one(p, carry):
            for index, slot, to_blk, to_head in targets:
                piece_copy(index, slot, p, to_blk, to_head).start()
            return carry

        lax.fori_loop(0, PIECES, one, 0)

    def sib_copy(index, slot):
        return pltpu.make_async_remote_copy(
            src_ref=keys.at[slot],
            dst_ref=keys.at[slot],
            send_sem=sib_send.at[index],
            recv_sem=sib_recv.at[slot],
            device_id={"blk": sibling, "head": head},
            device_id_type=MESH,
        )

    def to_sibling(slot):
        copy = sib_copy(len(whole), slot)
        copy.start()
        whole.append(copy)

    def w_copy(index, src, dst, to_blk):
        return pltpu.make_async_remote_copy(
            src_ref=src,
            dst_ref=dst,
            send_sem=w_send.at[index],
            recv_sem=w_recv.at[index],
            device_id={"blk": to_blk, "head": head},
            device_id_type=MESH,
        )

    carried = (yhi + x) % 2

    def carry_slot(step):
        return wrap_z(z + step) * 4 + carried * 2 + core

    def other_slot(step):
        return wrap_z(z + step) * 4 + (1 - carried) * 2 + core

    loads[0].wait()
    loads[1].wait()
    across, up, down = new_send(), new_send(), new_send()
    send_pieces((across, blk, other_y, head_y))

    @pl.when(x % 2 == 0)
    def _():
        send_pieces((up, blk, at_z(1), head), (down, blk, at_z(-1), head))

    to_sibling(blk)

    lane_max[...] = jnp.full_like(lane_max, -jnp.inf)
    top[...] = jnp.full_like(top, -jnp.inf)
    lane_sum[...] = jnp.zeros_like(lane_sum)
    acc[...] = jnp.zeros_like(acc)

    for index in (2, 3, 4):
        loads[index].wait()
    for h in range(heads):
        product = jnp.dot(qn[:, h * nope:(h + 1) * nope], ka[h], preferred_element_type=F32)
        queries[h * rows:(h + 1) * rows, 0:lat] = product.astype(BF16)
        queries[h * rows:(h + 1) * rows, lat:lat + rope] = qr[:, h * rope:(h + 1) * rope]

    def across_piece(p, carry):
        piece_wait(flip(blk, 2), p)

        @pl.when(x % 2 == 1)
        def _():
            piece_copy(up, flip(blk, 2), p, at_z(1), head).start()
            piece_copy(down, flip(blk, 2), p, at_z(-1), head).start()

        return carry

    lax.fori_loop(0, PIECES, across_piece, 0)
    to_sibling(flip(blk, 2))

    own_w = weight.at[mine]
    far = flip(mine, 2)
    loads[5].wait()
    w_sends = [w_copy(0, own_w, own_w, other_y), w_copy(1, own_w, own_w, sibling)]
    for copy in w_sends:
        copy.start()

    def units(*places):
        bases = [wrap_z(z + step) * 4 + half_y * 2 for step, half_y in places]
        for base in bases:
            sib_copy(0, base + 1 - core).wait_recv()
        block = jnp.concatenate([keys[base + k] for base in bases for k in range(2)], axis=1)
        product = jnp.dot(queries[...], block, preferred_element_type=F32)
        first, others = product[0:group_rows], product[group_rows:]
        turned = block[0:lat].T
        width = block.shape[1] // 4
        for k, base in enumerate(bases):
            scores[base // 2] = others[:, 2 * k * width:2 * (k + 1) * width]
            keys_t[base // 2] = turned[2 * k * width:2 * (k + 1) * width]
        largest = jnp.maximum(
            jnp.maximum(others[:, :width], others[:, width:2 * width]),
            jnp.maximum(others[:, 2 * width:3 * width], others[:, 3 * width:]),
        )
        lane_max[...] = jnp.maximum(lane_max[...], largest)
        before = top[...]
        now = jnp.maximum(before, jnp.max(first, axis=1, keepdims=True))
        shrink = jnp.exp2((before - now) * factor)
        value = jnp.exp2((first - jnp.concatenate([now] * 4, axis=1)) * factor)
        top[...] = now
        lane_sum[...] = lane_sum[...] * shrink + (
            (value[:, :width] + value[:, width:2 * width]) + (value[:, 2 * width:3 * width] + value[:, 3 * width:])
        )
        grown = jnp.dot(value.astype(BF16), turned, preferred_element_type=F32)
        acc[...] = acc[...] * jnp.concatenate([shrink] * (lat // width), axis=1) + grown

    def both(step, half_y):
        units((step, half_y), (-step, half_y))

    def advance(step):
        ways = (1, -1)
        forward = [new_send() for _ in ways] if step < 3 else [new_send()]
        along_x = [new_send() for _ in ways]

        def one(p, carry):
            for k, way in enumerate(ways):
                slot = carry_slot(-way * step)
                piece_wait(slot, p)
                if step < 3:
                    piece_copy(forward[k], slot, p, at_z(way), head).start()
            if step == 3:
                piece_copy(forward[0], carry_slot(-side * 3), p, at_z(side), head).start()
            for k, way in enumerate(ways):
                piece_copy(along_x[k], carry_slot(-way * step), p, blk, at_x(way)).start()
            return carry

        lax.fori_loop(0, PIECES, one, 0)
        for way in ways:
            to_sibling(carry_slot(-way * step))

    def others(step):
        for way in (1, -1):
            pieces_wait(other_slot(-way * step))
            to_sibling(other_slot(-way * step))

    advance(1)
    units((0, yhi), (0, 1 - yhi))
    advance(2)
    both(1, carried)
    advance(3)
    others(1)
    both(2, carried)
    last = new_send()

    def last_piece(p, carry):
        piece_wait(carry_slot(4), p)
        piece_copy(last, carry_slot(4), p, blk, at_x(side)).start()
        return carry

    lax.fori_loop(0, PIECES, last_piece, 0)
    to_sibling(carry_slot(4))
    others(2)
    both(1, 1 - carried)
    both(3, carried)
    others(3)
    both(2, 1 - carried)
    pieces_wait(other_slot(4))
    to_sibling(other_slot(4))
    both(3, 1 - carried)
    units((4, carried), (4, 1 - carried))

    att_sends = {}

    def att_copy(index, slot, group, to_blk):
        return pltpu.make_async_remote_copy(
            src_ref=att.at[slot, group],
            dst_ref=att.at[slot, group],
            send_sem=att_send.at[index],
            recv_sem=att_recv.at[slot, group],
            device_id={"blk": to_blk, "head": head},
            device_id_type=MESH,
        )

    def att_forward(step, group, way):
        copy = att_copy(len(att_sends), wrap_z(z - way * step), group, at_z(way))
        copy.start()
        att_sends[step, group, way] = copy

    def att_wait(slot, group):
        att_copy(0, slot, group, at_z(1)).wait_recv()

    def pass_on(step, group):
        for way in (1, -1):
            att_wait(wrap_z(z - way * step), group)
            if step < 3 or (group % 2 == 0) == (way == 1):
                att_forward(step, group, way)

    loads[6].wait()
    def mix(start):
        rows_at = pl.ds(start, group_rows)
        largest = jnp.max(lane_max[rows_at], axis=1, keepdims=True)
        weights, total = [], None
        for u in range(scores.shape[0]):
            value = jnp.exp2((scores[u, rows_at] - largest) * factor)
            weights.append(value.astype(BF16))
            width = value.shape[1] // 2
            value = value[:, :width] + value[:, width:]
            total = value if total is None else total + value
        mixed = jnp.dot(
            jnp.concatenate(weights, axis=1), keys_t[...].reshape(-1, lat), preferred_element_type=F32
        )
        return mixed, total

    for group in range(GROUPS):
        if group == 0:
            mixed, total = acc[...], lane_sum[...]
        else:
            mixed, total = mix((group - 1) * group_rows)
        mixture = (mixed / jnp.sum(total, axis=1, keepdims=True)).astype(BF16)
        for h in range(group_heads):
            value = jnp.dot(mixture[h * rows:(h + 1) * rows], va[group * group_heads + h], preferred_element_type=F32)
            att[z, group, :, h * vd:(h + 1) * vd] = value.astype(BF16)
        for way in (1, -1):
            att_forward(0, group, way)
        if group == 2:
            w_sends[0].wait_recv()
            w_sends.append(w_copy(2, weight.at[far], weight.at[far], sibling))
            w_sends[2].start()

    def out_copy(to_z, column):
        return pltpu.make_async_remote_copy(
            src_ref=part.at[to_z, column],
            dst_ref=summed.at[head * 4 + mine],
            send_sem=out_send.at[to_z * 4 + column],
            recv_sem=out_recv.at[head * 4 + mine],
            device_id={"blk": z * 4 + column, "head": to_z},
            device_id_type=MESH,
        )

    columns = out_ref.shape[0]
    rest = columns - 128
    strip = rows // 4
    spare = 128 - rest

    def pack(ref, value):
        ref[0:rows] = value[:, 0:128]
        for i in range(3):
            at = rows + i * strip
            ref[at:at + strip, 0:rest] = value[i * strip:(i + 1) * strip, 128:columns]
            ref[at:at + strip, rest:128] = value[3 * strip:rows, 128 + i * spare:128 + (i + 1) * spare]

    def project(slots):
        lhs = [jnp.concatenate([att[slot, group] for group in range(GROUPS)], axis=1) for slot in slots]
        lhs = jnp.concatenate(lhs, axis=0) if len(slots) > 1 else lhs[0]

        def one(column, carry):
            value = lax.dot_general(
                lhs, weight[column], (((1,), (1,)), ((), ())), preferred_element_type=F32
            ).astype(BF16)
            for k, slot in enumerate(slots):
                pack(part.at[slot, column], value[k * rows:(k + 1) * rows])
                here = jnp.logical_and(slot == head, column == mine)

                @pl.when(here)
                def _():
                    summed[head * 4 + mine] = part[slot, column]

                @pl.when(jnp.logical_not(here))
                def _():
                    out_copy(slot, column).start()

            return carry

        lax.fori_loop(0, 4, one, 0)

    pass_on(1, 0)
    w_sends[1].wait_recv()
    w_sends[2].wait_recv()
    project([z])
    for group in range(1, GROUPS):
        pass_on(1, group)
    project([wrap_z(z - 1), wrap_z(z + 1)])
    for step in (2, 3):
        for group in range(GROUPS):
            pass_on(step, group)
        project([wrap_z(z - step), wrap_z(z + step)])
    for group in range(GROUPS):
        att_wait(wrap_z(z + 4), group)
    project([wrap_z(z + 4)])

    def arrive(i, carry):
        @pl.when(i != head * 4 + mine)
        def _():
            pltpu.make_async_remote_copy(
                src_ref=part.at[0, 0],
                dst_ref=summed.at[i],
                send_sem=out_send.at[0],
                recv_sem=out_recv.at[i],
                device_id={"blk": sibling, "head": head},
                device_id_type=MESH,
            ).wait_recv()

        return carry

    lax.fori_loop(0, 32, arrive, 0)
    for k in range(4):
        total = summed[k].astype(F32)
        for h in range(1, 8):
            total = total + summed[4 * h + k].astype(F32)
        at = k * rows
        totals[at:at + rows, 0:128] = total[0:rows]
        for i in range(3):
            piece = total[rows + i * strip:rows + (i + 1) * strip]
            totals[at + i * strip:at + (i + 1) * strip, 128:columns] = piece[:, 0:rest]
            totals[at + 3 * strip:at + rows, 128 + i * spare:128 + (i + 1) * spare] = piece[:, rest:128]
    out_ref[...] = totals[...].T.astype(BF16)

    def left(i, carry):
        piece_copy(i // PIECES, blk, i % PIECES, sibling, head).wait_send()
        return carry

    lax.fori_loop(0, len(sends) * PIECES, left, 0)
    for copy in whole + w_sends + list(att_sends.values()):
        copy.wait_send()

    def leave(i, carry):
        to_z, column = i // 4, i % 4

        @pl.when(jnp.logical_or(to_z != head, column != mine))
        def _():
            out_copy(to_z, column).wait_send()

        return carry

    lax.fori_loop(0, 32, leave, 0)


def body(query_nope, query_rope, key_absorb, value_absorb, out_weight, latent_cache, rope_key):
    out_weight = out_weight.T
    rows = query_nope.shape[0]
    heads, nope, lat = key_absorb.shape
    rope, docs = rope_key.shape
    vd = value_absorb.shape[2]
    columns, depth = out_weight.shape
    pairs = heads * rows
    group_rows = pairs // GROUPS
    any_spec = pl.BlockSpec(memory_space=pl.ANY)
    dma = pltpu.SemaphoreType.DMA
    return pl.pallas_call(
        kernel,
        out_shape=jax.ShapeDtypeStruct((columns, 4 * rows), BF16),
        in_specs=[any_spec] * 7,
        out_specs=pl.BlockSpec(memory_space=pltpu.VMEM),
        scratch_shapes=[
            pltpu.VMEM((32, lat + rope, docs), BF16),
            pltpu.VMEM((16, 2 * docs, lat), BF16),
            pltpu.VMEM((pairs, lat + rope), BF16),
            pltpu.VMEM(query_nope.shape, BF16),
            pltpu.VMEM(query_rope.shape, BF16),
            pltpu.VMEM(key_absorb.shape, BF16),
            pltpu.VMEM(value_absorb.shape, BF16),
            pltpu.VMEM((4, columns, depth), BF16),
            pltpu.VMEM((16, pairs - group_rows, 2 * docs), F32),
            pltpu.VMEM((pairs - group_rows, docs), F32),
            pltpu.VMEM((group_rows, docs), F32),
            pltpu.VMEM((group_rows, docs), F32),
            pltpu.VMEM((group_rows, lat), F32),
            pltpu.VMEM((Z, GROUPS, rows, heads // GROUPS * vd), BF16),
            pltpu.VMEM((Z, 4, rows * columns // 128, 128), BF16),
            pltpu.VMEM((32, rows * columns // 128, 128), BF16),
            pltpu.VMEM((4 * rows, columns), F32),
            dma((7,)),
            dma((15, PIECES)),
            dma((32, PIECES)),
            dma((16,)),
            dma((32,)),
            dma((3,)),
            dma((3,)),
            dma((28,)),
            dma((Z, GROUPS)),
            dma((32,)),
            dma((32,)),
        ],
        compiler_params=pltpu.CompilerParams(
            collective_id=0, has_side_effects=True, vmem_limit_bytes=60 * 1024 * 1024
        ),
    )(query_nope, query_rope, key_absorb, value_absorb, out_weight, latent_cache, rope_key).T


def solution(mesh):
    in_specs = (
        P("blk", "head"),
        P("blk", "head"),
        P("head", None, None),
        P("head", None, None),
        P("head", "blk"),
        P(None, "blk"),
        P(None, "blk"),
    )
    return jax.shard_map(body, mesh=mesh, in_specs=in_specs, out_specs=P("head", "blk"), check_vma=False)
```

```python
import functools
import math

import jax
import jax.numpy as jnp
from jax import lax
from jax.experimental import pallas as pl
from jax.experimental.pallas import tpu as pltpu
from jax.sharding import PartitionSpec as P

MESH = pl.DeviceIdType.MESH
F32 = jnp.float32
BF16 = jnp.bfloat16

Z = 8
X = 4
GROUPS = 4
PIECES = 4


def flip(value, bit):
    return value + bit - 2 * bit * (value // bit % 2)


def kernel(
    qn_hbm, qr_hbm, ka_hbm, va_hbm, w_hbm, lat_hbm, rk_hbm, out_ref,
    keys, queries, qn, qr, ka, va, weight, top, lane_sum, acc,
    att, part, summed, totals,
    local_sem, key_send, key_recv, sib_send, sib_recv, w_send, w_recv, att_send, att_recv, out_send, out_recv,
):
    blk = lax.axis_index("blk")
    head = lax.axis_index("head")
    z = blk // 4
    mine = blk % 4
    yhi = mine // 2
    core = blk % 2
    x = head // 2
    sibling = flip(blk, 1)
    other_y = flip(blk, 2)
    head_y = flip(head, 1)
    side = 1 - 2 * core

    lat = lat_hbm.shape[0]
    rope = rk_hbm.shape[0]
    heads, nope = ka_hbm.shape[0], ka_hbm.shape[1]
    vd = va_hbm.shape[2]
    rows = qn_hbm.shape[0]
    group_heads = heads // GROUPS
    group_rows = group_heads * rows
    factor = (nope + rope) ** (-0.5) * math.log2(math.e)

    def wrap_z(value):
        return (value + 2 * Z) % Z

    def at_z(step):
        return wrap_z(z + step) * 4 + mine

    def at_x(step):
        return (x + step + X) % X * 2 + head % 2

    barrier = pltpu.get_barrier_semaphore()
    for step in (1, -1):
        pl.semaphore_signal(barrier, inc=1, device_id={"blk": at_z(step), "head": head}, device_id_type=MESH)

    for to_blk, to_head in ((blk, at_x(1)), (blk, at_x(-1)), (other_y, head_y), (other_y, head), (sibling, head)):
        pl.semaphore_signal(barrier, inc=1, device_id={"blk": to_blk, "head": to_head}, device_id_type=MESH)

    loads = [
        pltpu.make_async_copy(lat_hbm, keys.at[blk, pl.ds(0, lat)], local_sem.at[0]),
        pltpu.make_async_copy(rk_hbm, keys.at[blk, pl.ds(lat, rope)], local_sem.at[1]),
        pltpu.make_async_copy(qn_hbm, qn, local_sem.at[2]),
        pltpu.make_async_copy(qr_hbm, qr, local_sem.at[3]),
        pltpu.make_async_copy(ka_hbm, ka, local_sem.at[4]),
        pltpu.make_async_copy(w_hbm, weight.at[mine], local_sem.at[5]),
        pltpu.make_async_copy(va_hbm, va, local_sem.at[6]),
    ]
    for load in loads:
        load.start()

    pl.semaphore_wait(barrier, 7)

    depth = (lat + rope) // PIECES
    sends = []
    whole = []

    def piece_copy(index, slot, p, to_blk, to_head):
        at = keys.at[slot, pl.ds(pl.multiple_of(p * depth, 16), depth)]
        return pltpu.make_async_remote_copy(
            src_ref=at,
            dst_ref=at,
            send_sem=key_send.at[index, p],
            recv_sem=key_recv.at[slot, p],
            device_id={"blk": to_blk, "head": to_head},
            device_id_type=MESH,
        )

    def new_send():
        sends.append(None)
        return len(sends) - 1

    def piece_wait(slot, p):
        piece_copy(0, slot, p, sibling, head).wait_recv()

    def pieces_wait(slot):
        def one(p, carry):
            piece_wait(slot, p)
            return carry

        lax.fori_loop(0, PIECES, one, 0)

    def send_pieces(*targets):
        def one(p, carry):
            for index, slot, to_blk, to_head in targets:
                piece_copy(index, slot, p, to_blk, to_head).start()
            return carry

        lax.fori_loop(0, PIECES, one, 0)

    def sib_copy(index, slot):
        return pltpu.make_async_remote_copy(
            src_ref=keys.at[slot],
            dst_ref=keys.at[slot],
            send_sem=sib_send.at[index],
            recv_sem=sib_recv.at[slot],
            device_id={"blk": sibling, "head": head},
            device_id_type=MESH,
        )

    def to_sibling(slot):
        copy = sib_copy(len(whole), slot)
        copy.start()
        whole.append(copy)

    def w_copy(index, src, dst, to_blk):
        return pltpu.make_async_remote_copy(
            src_ref=src,
            dst_ref=dst,
            send_sem=w_send.at[index],
            recv_sem=w_recv.at[index],
            device_id={"blk": to_blk, "head": head},
            device_id_type=MESH,
        )

    carried = (yhi + x) % 2

    def carry_slot(step):
        return wrap_z(z + step) * 4 + carried * 2 + core

    def other_slot(step):
        return wrap_z(z + step) * 4 + (1 - carried) * 2 + core

    loads[0].wait()
    loads[1].wait()
    across, up, down = new_send(), new_send(), new_send()
    send_pieces((across, blk, other_y, head_y))

    @pl.when(x % 2 == 0)
    def _():
        send_pieces((up, blk, at_z(1), head), (down, blk, at_z(-1), head))

    to_sibling(blk)

    top[...] = jnp.full_like(top, -jnp.inf)
    lane_sum[...] = jnp.zeros_like(lane_sum)
    acc[...] = jnp.zeros_like(acc)

    for index in (2, 3, 4):
        loads[index].wait()
    for h in range(heads):
        product = jnp.dot(qn[:, h * nope:(h + 1) * nope], ka[h], preferred_element_type=F32)
        queries[h * rows:(h + 1) * rows, 0:lat] = product.astype(BF16)
        queries[h * rows:(h + 1) * rows, lat:lat + rope] = qr[:, h * rope:(h + 1) * rope]

    def across_piece(p, carry):
        piece_wait(flip(blk, 2), p)

        @pl.when(x % 2 == 1)
        def _():
            piece_copy(up, flip(blk, 2), p, at_z(1), head).start()
            piece_copy(down, flip(blk, 2), p, at_z(-1), head).start()

        return carry

    lax.fori_loop(0, PIECES, across_piece, 0)
    to_sibling(flip(blk, 2))

    own_w = weight.at[mine]
    far = flip(mine, 2)
    loads[5].wait()
    w_sends = [w_copy(0, own_w, own_w, other_y), w_copy(1, own_w, own_w, sibling)]
    for copy in w_sends:
        copy.start()

    def units(*places):
        bases = [wrap_z(z + step) * 4 + half_y * 2 for step, half_y in places]
        for base in bases:
            sib_copy(0, base + 1 - core).wait_recv()
        block = jnp.concatenate([keys[base + k] for base in bases for k in range(2)], axis=1)
        first = jnp.dot(queries[...], block, preferred_element_type=F32)
        turned = block[0:lat].T
        width = block.shape[1] // 4
        before = top[...]
        now = jnp.maximum(before, jnp.max(first, axis=1, keepdims=True))
        shrink = jnp.exp2((before - now) * factor)
        value = jnp.exp2((first - jnp.concatenate([now] * 4, axis=1)) * factor)
        top[...] = now
        lane_sum[...] = lane_sum[...] * shrink + (
            (value[:, :width] + value[:, width:2 * width]) + (value[:, 2 * width:3 * width] + value[:, 3 * width:])
        )
        grown = jnp.dot(value.astype(BF16), turned, preferred_element_type=F32)
        acc[...] = acc[...] * jnp.concatenate([shrink] * (lat // width), axis=1) + grown

    def both(step, half_y):
        units((step, half_y), (-step, half_y))

    def advance(step):
        ways = (1, -1)
        forward = [new_send() for _ in ways] if step < 3 else [new_send()]
        along_x = [new_send() for _ in ways]

        def one(p, carry):
            for k, way in enumerate(ways):
                slot = carry_slot(-way * step)
                piece_wait(slot, p)
                if step < 3:
                    piece_copy(forward[k], slot, p, at_z(way), head).start()
            if step == 3:
                piece_copy(forward[0], carry_slot(-side * 3), p, at_z(side), head).start()
            for k, way in enumerate(ways):
                piece_copy(along_x[k], carry_slot(-way * step), p, blk, at_x(way)).start()
            return carry

        lax.fori_loop(0, PIECES, one, 0)
        for way in ways:
            to_sibling(carry_slot(-way * step))

    def others(step):
        for way in (1, -1):
            pieces_wait(other_slot(-way * step))
            to_sibling(other_slot(-way * step))

    advance(1)
    units((0, yhi), (0, 1 - yhi))
    advance(2)
    both(1, carried)
    advance(3)
    others(1)
    both(2, carried)
    last = new_send()

    def last_piece(p, carry):
        piece_wait(carry_slot(4), p)
        piece_copy(last, carry_slot(4), p, blk, at_x(side)).start()
        return carry

    lax.fori_loop(0, PIECES, last_piece, 0)
    to_sibling(carry_slot(4))
    others(2)
    both(1, 1 - carried)
    both(3, carried)
    others(3)
    both(2, 1 - carried)
    pieces_wait(other_slot(4))
    to_sibling(other_slot(4))
    both(3, 1 - carried)
    units((4, carried), (4, 1 - carried))

    att_sends = {}

    def att_copy(index, slot, group, to_blk):
        return pltpu.make_async_remote_copy(
            src_ref=att.at[slot, group],
            dst_ref=att.at[slot, group],
            send_sem=att_send.at[index],
            recv_sem=att_recv.at[slot, group],
            device_id={"blk": to_blk, "head": head},
            device_id_type=MESH,
        )

    def att_forward(step, group, way):
        copy = att_copy(len(att_sends), wrap_z(z - way * step), group, at_z(way))
        copy.start()
        att_sends[step, group, way] = copy

    def att_wait(slot, group):
        att_copy(0, slot, group, at_z(1)).wait_recv()

    def pass_on(step, group):
        for way in (1, -1):
            att_wait(wrap_z(z - way * step), group)
            if step < 3 or (group % 2 == 0) == (way == 1):
                att_forward(step, group, way)

    loads[6].wait()
    for group in range(GROUPS):
        rows_at = pl.ds(group * group_rows, group_rows)
        mixed, total = acc[rows_at], lane_sum[rows_at]
        mixture = (mixed / jnp.sum(total, axis=1, keepdims=True)).astype(BF16)
        for h in range(group_heads):
            value = jnp.dot(mixture[h * rows:(h + 1) * rows], va[group * group_heads + h], preferred_element_type=F32)
            att[z, group, :, h * vd:(h + 1) * vd] = value.astype(BF16)
        for way in (1, -1):
            att_forward(0, group, way)
        if group == 2:
            w_sends[0].wait_recv()
            w_sends.append(w_copy(2, weight.at[far], weight.at[far], sibling))
            w_sends[2].start()

    def out_copy(to_z, column):
        return pltpu.make_async_remote_copy(
            src_ref=part.at[to_z, column],
            dst_ref=summed.at[head * 4 + mine],
            send_sem=out_send.at[to_z * 4 + column],
            recv_sem=out_recv.at[head * 4 + mine],
            device_id={"blk": z * 4 + column, "head": to_z},
            device_id_type=MESH,
        )

    columns = out_ref.shape[0]
    rest = columns - 128
    strip = rows // 4
    spare = 128 - rest

    def pack(ref, value):
        ref[0:rows] = value[:, 0:128]
        for i in range(3):
            at = rows + i * strip
            ref[at:at + strip, 0:rest] = value[i * strip:(i + 1) * strip, 128:columns]
            ref[at:at + strip, rest:128] = value[3 * strip:rows, 128 + i * spare:128 + (i + 1) * spare]

    def project(slots):
        lhs = [jnp.concatenate([att[slot, group] for group in range(GROUPS)], axis=1) for slot in slots]
        lhs = jnp.concatenate(lhs, axis=0) if len(slots) > 1 else lhs[0]

        def one(column, carry):
            value = lax.dot_general(
                lhs, weight[column], (((1,), (1,)), ((), ())), preferred_element_type=F32
            ).astype(BF16)
            for k, slot in enumerate(slots):
                pack(part.at[slot, column], value[k * rows:(k + 1) * rows])
                here = jnp.logical_and(slot == head, column == mine)

                @pl.when(here)
                def _():
                    summed[head * 4 + mine] = part[slot, column]

                @pl.when(jnp.logical_not(here))
                def _():
                    out_copy(slot, column).start()

            return carry

        lax.fori_loop(0, 4, one, 0)

    pass_on(1, 0)
    w_sends[1].wait_recv()
    w_sends[2].wait_recv()
    project([z])
    for group in range(1, GROUPS):
        pass_on(1, group)
    project([wrap_z(z - 1), wrap_z(z + 1)])
    for step in (2, 3):
        for group in range(GROUPS):
            pass_on(step, group)
        project([wrap_z(z - step), wrap_z(z + step)])
    for group in range(GROUPS):
        att_wait(wrap_z(z + 4), group)
    project([wrap_z(z + 4)])

    def arrive(i, carry):
        @pl.when(i != head * 4 + mine)
        def _():
            pltpu.make_async_remote_copy(
                src_ref=part.at[0, 0],
                dst_ref=summed.at[i],
                send_sem=out_send.at[0],
                recv_sem=out_recv.at[i],
                device_id={"blk": sibling, "head": head},
                device_id_type=MESH,
            ).wait_recv()

        return carry

    lax.fori_loop(0, 32, arrive, 0)
    for k in range(4):
        total = summed[k].astype(F32)
        for h in range(1, 8):
            total = total + summed[4 * h + k].astype(F32)
        at = k * rows
        totals[at:at + rows, 0:128] = total[0:rows]
        for i in range(3):
            piece = total[rows + i * strip:rows + (i + 1) * strip]
            totals[at + i * strip:at + (i + 1) * strip, 128:columns] = piece[:, 0:rest]
            totals[at + 3 * strip:at + rows, 128 + i * spare:128 + (i + 1) * spare] = piece[:, rest:128]
    out_ref[...] = totals[...].T.astype(BF16)

    def left(i, carry):
        piece_copy(i // PIECES, blk, i % PIECES, sibling, head).wait_send()
        return carry

    lax.fori_loop(0, len(sends) * PIECES, left, 0)
    for copy in whole + w_sends + list(att_sends.values()):
        copy.wait_send()

    def leave(i, carry):
        to_z, column = i // 4, i % 4

        @pl.when(jnp.logical_or(to_z != head, column != mine))
        def _():
            out_copy(to_z, column).wait_send()

        return carry

    lax.fori_loop(0, 32, leave, 0)


def body(query_nope, query_rope, key_absorb, value_absorb, out_weight, latent_cache, rope_key):
    out_weight = out_weight.T
    rows = query_nope.shape[0]
    heads, nope, lat = key_absorb.shape
    rope, docs = rope_key.shape
    vd = value_absorb.shape[2]
    columns, depth = out_weight.shape
    pairs = heads * rows
    any_spec = pl.BlockSpec(memory_space=pl.ANY)
    dma = pltpu.SemaphoreType.DMA
    return pl.pallas_call(
        kernel,
        out_shape=jax.ShapeDtypeStruct((columns, 4 * rows), BF16),
        in_specs=[any_spec] * 7,
        out_specs=pl.BlockSpec(memory_space=pltpu.VMEM),
        scratch_shapes=[
            pltpu.VMEM((32, lat + rope, docs), BF16),
            pltpu.VMEM((pairs, lat + rope), BF16),
            pltpu.VMEM(query_nope.shape, BF16),
            pltpu.VMEM(query_rope.shape, BF16),
            pltpu.VMEM(key_absorb.shape, BF16),
            pltpu.VMEM(value_absorb.shape, BF16),
            pltpu.VMEM((4, columns, depth), BF16),
            pltpu.VMEM((pairs, docs), F32),
            pltpu.VMEM((pairs, docs), F32),
            pltpu.VMEM((pairs, lat), F32),
            pltpu.VMEM((Z, GROUPS, rows, heads // GROUPS * vd), BF16),
            pltpu.VMEM((Z, 4, rows * columns // 128, 128), BF16),
            pltpu.VMEM((32, rows * columns // 128, 128), BF16),
            pltpu.VMEM((4 * rows, columns), F32),
            dma((7,)),
            dma((15, PIECES)),
            dma((32, PIECES)),
            dma((16,)),
            dma((32,)),
            dma((3,)),
            dma((3,)),
            dma((28,)),
            dma((Z, GROUPS)),
            dma((32,)),
            dma((32,)),
        ],
        compiler_params=pltpu.CompilerParams(
            collective_id=0, has_side_effects=True, vmem_limit_bytes=60 * 1024 * 1024
        ),
    )(query_nope, query_rope, key_absorb, value_absorb, out_weight, latent_cache, rope_key).T


def solution(mesh):
    in_specs = (
        P("blk", "head"),
        P("blk", "head"),
        P("head", None, None),
        P("head", None, None),
        P("head", "blk"),
        P(None, "blk"),
        P(None, "blk"),
    )
    return jax.shard_map(body, mesh=mesh, in_specs=in_specs, out_specs=P("head", "blk"), check_vma=False)
```

```python
import functools
import math

import jax
import jax.numpy as jnp
from jax import lax
from jax.experimental import pallas as pl
from jax.experimental.pallas import tpu as pltpu
from jax.sharding import PartitionSpec as P

MESH = pl.DeviceIdType.MESH
F32 = jnp.float32
BF16 = jnp.bfloat16

Z = 8
X = 4
GROUPS = 4
PIECES = 4


def flip(value, bit):
    return value + bit - 2 * bit * (value // bit % 2)


def kernel(
    qn_hbm, qr_hbm, ka_hbm, va_hbm, w_hbm, lat_hbm, rk_hbm, out_ref,
    keys, queries, qn, qr, ka, va, weight, top, lane_sum, acc,
    att, part, summed, totals,
    local_sem, key_send, key_recv, sib_send, sib_recv, w_send, w_recv, att_send, att_recv, out_send, out_recv,
):
    blk = lax.axis_index("blk")
    head = lax.axis_index("head")
    z = blk // 4
    mine = blk % 4
    yhi = mine // 2
    core = blk % 2
    x = head // 2
    sibling = flip(blk, 1)
    other_y = flip(blk, 2)
    head_y = flip(head, 1)
    side = 1 - 2 * core

    lat = lat_hbm.shape[0]
    rope = rk_hbm.shape[0]
    heads, nope = ka_hbm.shape[0], ka_hbm.shape[1]
    vd = va_hbm.shape[2]
    rows = qn_hbm.shape[0]
    group_heads = heads // GROUPS
    group_rows = group_heads * rows
    factor = (nope + rope) ** (-0.5) * math.log2(math.e)

    def wrap_z(value):
        return (value + 2 * Z) % Z

    def at_z(step):
        return wrap_z(z + step) * 4 + mine

    def at_x(step):
        return (x + step + X) % X * 2 + head % 2

    barrier = pltpu.get_barrier_semaphore()
    for step in (1, -1):
        pl.semaphore_signal(barrier, inc=1, device_id={"blk": at_z(step), "head": head}, device_id_type=MESH)

    for to_blk, to_head in ((blk, at_x(1)), (blk, at_x(-1)), (other_y, head_y), (other_y, head), (sibling, head)):
        pl.semaphore_signal(barrier, inc=1, device_id={"blk": to_blk, "head": to_head}, device_id_type=MESH)

    loads = [
        pltpu.make_async_copy(lat_hbm, keys.at[blk, pl.ds(0, lat)], local_sem.at[0]),
        pltpu.make_async_copy(rk_hbm, keys.at[blk, pl.ds(lat, rope)], local_sem.at[1]),
        pltpu.make_async_copy(qn_hbm, qn, local_sem.at[2]),
        pltpu.make_async_copy(qr_hbm, qr, local_sem.at[3]),
        pltpu.make_async_copy(ka_hbm, ka, local_sem.at[4]),
        pltpu.make_async_copy(w_hbm, weight.at[mine], local_sem.at[5]),
        pltpu.make_async_copy(va_hbm, va, local_sem.at[6]),
    ]
    for load in loads:
        load.start()

    pl.semaphore_wait(barrier, 7)

    depth = (lat + rope) // PIECES
    sends = []
    whole = []

    def piece_copy(index, slot, p, to_blk, to_head):
        at = keys.at[slot, pl.ds(pl.multiple_of(p * depth, 16), depth)]
        return pltpu.make_async_remote_copy(
            src_ref=at,
            dst_ref=at,
            send_sem=key_send.at[index, p],
            recv_sem=key_recv.at[slot, p],
            device_id={"blk": to_blk, "head": to_head},
            device_id_type=MESH,
        )

    def new_send():
        sends.append(None)
        return len(sends) - 1

    def piece_wait(slot, p):
        piece_copy(0, slot, p, sibling, head).wait_recv()

    def pieces_wait(slot):
        def one(p, carry):
            piece_wait(slot, p)
            return carry

        lax.fori_loop(0, PIECES, one, 0)

    def send_pieces(*targets):
        def one(p, carry):
            for index, slot, to_blk, to_head in targets:
                piece_copy(index, slot, p, to_blk, to_head).start()
            return carry

        lax.fori_loop(0, PIECES, one, 0)

    def sib_copy(index, slot):
        return pltpu.make_async_remote_copy(
            src_ref=keys.at[slot],
            dst_ref=keys.at[slot],
            send_sem=sib_send.at[index],
            recv_sem=sib_recv.at[slot],
            device_id={"blk": sibling, "head": head},
            device_id_type=MESH,
        )

    def to_sibling(slot):
        copy = sib_copy(len(whole), slot)
        copy.start()
        whole.append(copy)

    def w_copy(index, src, dst, to_blk):
        return pltpu.make_async_remote_copy(
            src_ref=src,
            dst_ref=dst,
            send_sem=w_send.at[index],
            recv_sem=w_recv.at[index],
            device_id={"blk": to_blk, "head": head},
            device_id_type=MESH,
        )

    carried = (yhi + x) % 2

    def carry_slot(step):
        return wrap_z(z + step) * 4 + carried * 2 + core

    def other_slot(step):
        return wrap_z(z + step) * 4 + (1 - carried) * 2 + core

    loads[0].wait()
    loads[1].wait()
    across, up, down = new_send(), new_send(), new_send()
    send_pieces((across, blk, other_y, head_y))

    @pl.when(x % 2 == 0)
    def _():
        send_pieces((up, blk, at_z(1), head), (down, blk, at_z(-1), head))

    to_sibling(blk)

    top[...] = jnp.full_like(top, -jnp.inf)
    lane_sum[...] = jnp.zeros_like(lane_sum)
    acc[...] = jnp.zeros_like(acc)

    for index in (2, 3, 4):
        loads[index].wait()
    for h in range(heads):
        product = jnp.dot(qn[:, h * nope:(h + 1) * nope], ka[h], preferred_element_type=F32)
        queries[h * rows:(h + 1) * rows, 0:lat] = product.astype(BF16)
        queries[h * rows:(h + 1) * rows, lat:lat + rope] = qr[:, h * rope:(h + 1) * rope]

    def across_piece(p, carry):
        piece_wait(flip(blk, 2), p)

        @pl.when(x % 2 == 1)
        def _():
            piece_copy(up, flip(blk, 2), p, at_z(1), head).start()
            piece_copy(down, flip(blk, 2), p, at_z(-1), head).start()

        return carry

    lax.fori_loop(0, PIECES, across_piece, 0)
    to_sibling(flip(blk, 2))

    own_w = weight.at[mine]
    far = flip(mine, 2)
    loads[5].wait()
    w_sends = [w_copy(0, own_w, own_w, other_y), w_copy(1, own_w, own_w, sibling)]
    for copy in w_sends:
        copy.start()

    def units(*places):
        bases = [wrap_z(z + step) * 4 + half_y * 2 for step, half_y in places]
        for base in bases:
            sib_copy(0, base + 1 - core).wait_recv()
        block = jnp.concatenate([keys[base + k] for base in bases for k in range(2)], axis=1)
        first = jnp.dot(queries[...], block, preferred_element_type=F32)
        turned = block[0:lat].T
        width = block.shape[1] // 4
        before = top[...]
        now = jnp.maximum(before, jnp.max(first, axis=1, keepdims=True))
        shrink = jnp.exp2((before - now) * factor)
        value = jnp.exp2((first - jnp.concatenate([now] * 4, axis=1)) * factor)
        top[...] = now
        lane_sum[...] = lane_sum[...] * shrink + (
            (value[:, :width] + value[:, width:2 * width]) + (value[:, 2 * width:3 * width] + value[:, 3 * width:])
        )
        grown = jnp.dot(value.astype(BF16), turned, preferred_element_type=F32)
        acc[...] = acc[...] * jnp.concatenate([shrink] * (lat // width), axis=1) + grown

    def both(step, half_y):
        units((step, half_y), (-step, half_y))

    def advance(step):
        ways = (1, -1)
        forward = [new_send() for _ in ways] if step < 3 else [new_send()]
        along_x = [new_send() for _ in ways]

        def one(p, carry):
            for k, way in enumerate(ways):
                slot = carry_slot(-way * step)
                piece_wait(slot, p)
                if step < 3:
                    piece_copy(forward[k], slot, p, at_z(way), head).start()
            if step == 3:
                piece_copy(forward[0], carry_slot(-side * 3), p, at_z(side), head).start()
            for k, way in enumerate(ways):
                piece_copy(along_x[k], carry_slot(-way * step), p, blk, at_x(way)).start()
            return carry

        lax.fori_loop(0, PIECES, one, 0)
        for way in ways:
            to_sibling(carry_slot(-way * step))

    def others(step):
        for way in (1, -1):
            pieces_wait(other_slot(-way * step))
            to_sibling(other_slot(-way * step))

    advance(1)
    units((0, yhi), (0, 1 - yhi))
    advance(2)
    both(1, carried)
    advance(3)
    others(1)
    both(2, carried)
    last = new_send()

    def last_piece(p, carry):
        piece_wait(carry_slot(4), p)
        piece_copy(last, carry_slot(4), p, blk, at_x(side)).start()
        return carry

    lax.fori_loop(0, PIECES, last_piece, 0)
    to_sibling(carry_slot(4))
    others(2)
    both(1, 1 - carried)
    both(3, carried)
    others(3)
    both(2, 1 - carried)
    pieces_wait(other_slot(4))
    to_sibling(other_slot(4))
    both(3, 1 - carried)
    units((4, carried), (4, 1 - carried))

    att_sends = {}

    def att_copy(index, slot, group, to_blk):
        return pltpu.make_async_remote_copy(
            src_ref=att.at[slot, group],
            dst_ref=att.at[slot, group],
            send_sem=att_send.at[index],
            recv_sem=att_recv.at[slot, group],
            device_id={"blk": to_blk, "head": head},
            device_id_type=MESH,
        )

    def att_forward(step, group, way):
        copy = att_copy(len(att_sends), wrap_z(z - way * step), group, at_z(way))
        copy.start()
        att_sends[step, group, way] = copy

    def att_wait(slot, group):
        att_copy(0, slot, group, at_z(1)).wait_recv()

    def pass_on(step, group):
        for way in (1, -1):
            att_wait(wrap_z(z - way * step), group)
            if step < 3 or (group % 2 == 0) == (way == 1):
                att_forward(step, group, way)

    loads[6].wait()
    for group in range(GROUPS):
        rows_at = pl.ds(group * group_rows, group_rows)
        mixed, total = acc[rows_at], lane_sum[rows_at]
        mixture = (mixed / jnp.sum(total, axis=1, keepdims=True)).astype(BF16)
        for h in range(group_heads):
            value = jnp.dot(mixture[h * rows:(h + 1) * rows], va[group * group_heads + h], preferred_element_type=F32)
            att[z, group, :, h * vd:(h + 1) * vd] = value.astype(BF16)
        for way in (1, -1):
            att_forward(0, group, way)
        if group == 2:
            w_sends[0].wait_recv()
            w_sends.append(w_copy(2, weight.at[far], weight.at[far], sibling))
            w_sends[2].start()

    def out_copy(to_z, column):
        return pltpu.make_async_remote_copy(
            src_ref=part.at[to_z, column],
            dst_ref=summed.at[head * 4 + mine],
            send_sem=out_send.at[to_z * 4 + column],
            recv_sem=out_recv.at[head * 4 + mine],
            device_id={"blk": z * 4 + column, "head": to_z},
            device_id_type=MESH,
        )

    columns = out_ref.shape[0]
    rest = columns - 128
    strip = rows // 4
    spare = 128 - rest

    def pack(ref, value):
        ref[0:rows] = value[:, 0:128]
        for i in range(3):
            at = rows + i * strip
            ref[at:at + strip, 0:rest] = value[i * strip:(i + 1) * strip, 128:columns]
            ref[at:at + strip, rest:128] = value[3 * strip:rows, 128 + i * spare:128 + (i + 1) * spare]

    def project(slots):
        lhs = [jnp.concatenate([att[slot, group] for group in range(GROUPS)], axis=1) for slot in slots]
        lhs = jnp.concatenate(lhs, axis=0) if len(slots) > 1 else lhs[0]

        def one(column, carry):
            value = lax.dot_general(
                lhs, weight[column], (((1,), (1,)), ((), ())), preferred_element_type=F32
            ).astype(BF16)
            for k, slot in enumerate(slots):
                pack(part.at[slot, column], value[k * rows:(k + 1) * rows])
                here = jnp.logical_and(slot == head, column == mine)

                @pl.when(here)
                def _():
                    summed[head * 4 + mine] = part[slot, column]

                @pl.when(jnp.logical_not(here))
                def _():
                    out_copy(slot, column).start()

            return carry

        lax.fori_loop(0, 4, one, 0)

    w_sends[1].wait_recv()
    w_sends[2].wait_recv()
    project([z])
    for group in range(GROUPS):
        pass_on(1, group)
    project([wrap_z(z - 1), wrap_z(z + 1)])
    for step in (2, 3):
        for group in range(GROUPS):
            pass_on(step, group)
        project([wrap_z(z - step), wrap_z(z + step)])
    for group in range(GROUPS):
        att_wait(wrap_z(z + 4), group)
    project([wrap_z(z + 4)])

    def arrive(i, carry):
        @pl.when(i != head * 4 + mine)
        def _():
            pltpu.make_async_remote_copy(
                src_ref=part.at[0, 0],
                dst_ref=summed.at[i],
                send_sem=out_send.at[0],
                recv_sem=out_recv.at[i],
                device_id={"blk": sibling, "head": head},
                device_id_type=MESH,
            ).wait_recv()

        return carry

    lax.fori_loop(0, 32, arrive, 0)
    for k in range(4):
        total = summed[k].astype(F32)
        for h in range(1, 8):
            total = total + summed[4 * h + k].astype(F32)
        at = k * rows
        totals[at:at + rows, 0:128] = total[0:rows]
        for i in range(3):
            piece = total[rows + i * strip:rows + (i + 1) * strip]
            totals[at + i * strip:at + (i + 1) * strip, 128:columns] = piece[:, 0:rest]
            totals[at + 3 * strip:at + rows, 128 + i * spare:128 + (i + 1) * spare] = piece[:, rest:128]
    out_ref[...] = totals[...].T.astype(BF16)

    def left(i, carry):
        piece_copy(i // PIECES, blk, i % PIECES, sibling, head).wait_send()
        return carry

    lax.fori_loop(0, len(sends) * PIECES, left, 0)
    for copy in whole + w_sends + list(att_sends.values()):
        copy.wait_send()

    def leave(i, carry):
        to_z, column = i // 4, i % 4

        @pl.when(jnp.logical_or(to_z != head, column != mine))
        def _():
            out_copy(to_z, column).wait_send()

        return carry

    lax.fori_loop(0, 32, leave, 0)


def body(query_nope, query_rope, key_absorb, value_absorb, out_weight, latent_cache, rope_key):
    out_weight = out_weight.T
    rows = query_nope.shape[0]
    heads, nope, lat = key_absorb.shape
    rope, docs = rope_key.shape
    vd = value_absorb.shape[2]
    columns, depth = out_weight.shape
    pairs = heads * rows
    any_spec = pl.BlockSpec(memory_space=pl.ANY)
    dma = pltpu.SemaphoreType.DMA
    return pl.pallas_call(
        kernel,
        out_shape=jax.ShapeDtypeStruct((columns, 4 * rows), BF16),
        in_specs=[any_spec] * 7,
        out_specs=pl.BlockSpec(memory_space=pltpu.VMEM),
        scratch_shapes=[
            pltpu.VMEM((32, lat + rope, docs), BF16),
            pltpu.VMEM((pairs, lat + rope), BF16),
            pltpu.VMEM(query_nope.shape, BF16),
            pltpu.VMEM(query_rope.shape, BF16),
            pltpu.VMEM(key_absorb.shape, BF16),
            pltpu.VMEM(value_absorb.shape, BF16),
            pltpu.VMEM((4, columns, depth), BF16),
            pltpu.VMEM((pairs, docs), F32),
            pltpu.VMEM((pairs, docs), F32),
            pltpu.VMEM((pairs, lat), F32),
            pltpu.VMEM((Z, GROUPS, rows, heads // GROUPS * vd), BF16),
            pltpu.VMEM((Z, 4, rows * columns // 128, 128), BF16),
            pltpu.VMEM((32, rows * columns // 128, 128), BF16),
            pltpu.VMEM((4 * rows, columns), F32),
            dma((7,)),
            dma((15, PIECES)),
            dma((32, PIECES)),
            dma((16,)),
            dma((32,)),
            dma((3,)),
            dma((3,)),
            dma((28,)),
            dma((Z, GROUPS)),
            dma((32,)),
            dma((32,)),
        ],
        compiler_params=pltpu.CompilerParams(
            collective_id=0, has_side_effects=True, vmem_limit_bytes=60 * 1024 * 1024
        ),
    )(query_nope, query_rope, key_absorb, value_absorb, out_weight, latent_cache, rope_key).T


def solution(mesh):
    in_specs = (
        P("blk", "head"),
        P("blk", "head"),
        P("head", None, None),
        P("head", None, None),
        P("head", "blk"),
        P(None, "blk"),
        P(None, "blk"),
    )
    return jax.shard_map(body, mesh=mesh, in_specs=in_specs, out_specs=P("head", "blk"), check_vma=False)
```
